512 devices in a mesh: grp: 32 (over y, x, core), sp: 16 (over z).
Axes of the slice: x: 4, y: 4, z: 16, core: 2. Of those that a mesh axis runs over, the one named last changes fastest.
Arguments:
- hidden: bfloat16 [128, 32, 65536], P(None, 'grp', 'sp'), may hold values from -6 to 6
- queries: bfloat16 [128, 32, 32768], P(None, 'grp', 'sp'), may hold values from -210 to 210
- key_weight: bfloat16 [4096, 512], P('sp'), may hold values from -0.09375 to 0.09375
- value_weight: bfloat16 [4096, 512], P('sp'), may hold values from -0.09375 to 0.09375
- lengths: int32 [64], replicated, may hold values from 512 to 2560, as said below
- assign: int32 [64], replicated, may hold values from 0 to 31, as said below
Outputs:
- attended: bfloat16 [32, 192, 32768], P('grp', None, 'sp')
The draws below stay inside these ranges and needn't reach their ends.
Inputs may be any that keep to these rules, and one draw needn't show every extreme that they name: Every length is a multiple of 512, and the lengths add up to 65536. `assign`: every group holds exactly two sequences, whose lengths add up to at most 3072 tokens; some group holds exactly that many.
All inputs are finite; a program needn't handle non-finite values.
Results may differ from the reference program's by a relative error of at most 0.011.
Values may be sent and summed in bfloat16 or wider, within the bound.
A program may use at most 64 MiB of HBM per device.

```python
import jax
import jax.numpy as jnp
from jax import lax

D = 4096
H = 16
KVH = 4
HD = 128
TOK_DEV = 128
SLOTS = 192
NSEQ = 64
N_GRP = 32
N_SP = 16


def sequence_plan(key):
    half_groups = N_GRP // 2
    mean_load = TOK_DEV // N_GRP
    full_load = 2 * mean_load - 2
    key_load, key_split, key_shuffle = jax.random.split(key, 3)
    loads = jax.random.randint(key_load, (half_groups,), 2, full_load + 1)
    loads = loads.at[0].set(full_load)
    loads = jnp.concatenate([loads, 2 * mean_load - loads])
    firsts = jax.random.randint(key_split, (N_GRP,), 1, loads)
    firsts = firsts.at[0].set(full_load - 1)
    seconds = loads - firsts
    sizes_all = jnp.concatenate([firsts, seconds]).astype(jnp.int32)
    owners = jnp.concatenate([jnp.arange(N_GRP), jnp.arange(N_GRP)]).astype(jnp.int32)
    shuffle = jax.random.permutation(key_shuffle, 2 * N_GRP)
    return ((sizes_all[shuffle] * (N_GRP * N_SP)).astype(jnp.int32), owners[shuffle])


def draw_lengths(key, part):
    lengths, owners = sequence_plan(key)
    return lengths


def draw_assign(key, part):
    lengths, owners = sequence_plan(key)
    return owners


def draw_queries(key, part):
    key = jax.random.fold_in(key, 7)
    full_shape = (TOK_DEV, N_GRP, N_SP * H * HD)
    return jax.random.normal(key, full_shape, jnp.float32).astype(jnp.bfloat16)


def shard_levels(stream_key, dims, pieces, low, high):
    gain = 1.0
    for dim, shards_of in pieces:
        draws = jax.random.uniform(jax.random.fold_in(jax.random.fold_in(stream_key, 6), dim), (shards_of,), jnp.float32, low / len(pieces), high / len(pieces))
        gain = gain * jnp.repeat(jnp.exp(draws), dims[dim] // shards_of).reshape((-1,) + (1,) * (len(dims) - 1 - dim))
    return gain


def scatter_about(rng, dims, deviation, limit, shards=(), kind=jnp.bfloat16):
    values = jax.random.normal(rng, dims, jnp.float32) * deviation
    if len(shards) > 0:
        values = shard_levels(rng, dims, shards, -0.22, 0.18) * values
    return jnp.clip(values, min=-limit, max=limit).astype(kind)


def setup_inputs(seed: int = 0) -> dict:
    splits = jax.random.split(jax.random.key(seed), 7)
    return {
        "hidden": scatter_about(splits[0], (TOK_DEV, N_GRP, N_SP * D), 1.0, 6.0, ((1, 32), (2, 16))),
        "queries": draw_queries(jax.random.fold_in(splits[6], 71), 0),
        "key_weight": scatter_about(splits[2], (D, KVH * HD), D ** -0.5, 0.09375, ((0, 16),)),
        "value_weight": scatter_about(splits[3], (D, KVH * HD), D ** -0.5, 0.09375, ((0, 16),)),
        "lengths": draw_lengths(jax.random.fold_in(splits[6], 71), 0),
        "assign": draw_assign(jax.random.fold_in(splits[6], 71), 0),
    }


ROPE_BASE = 500000.0
NEG_FILL = -1e30


def rotate(key_sum, positions):
    head_width = key_sum.shape[-1]
    half_width = head_width // 2
    frequency = ROPE_BASE ** (-2.0 * jnp.arange(half_width, dtype=jnp.float32) / head_width)
    angles = positions.astype(jnp.float32)[:, None] * frequency[None, :]
    cosine = jnp.cos(angles)[:, None, :]
    sine_part = jnp.sin(angles)[:, None, :]
    first_half = key_sum[..., :half_width]
    second_half = key_sum[..., half_width:]
    return jnp.concatenate([first_half * cosine - second_half * sine_part, second_half * cosine + first_half * sine_part], axis=-1)


def layout(lengths, assign):
    counts = (lengths // (N_GRP * N_SP)).astype(jnp.int32)
    starts = (jnp.cumsum(counts) - counts).astype(jnp.int32)
    seq_ids = jnp.arange(NSEQ, dtype=jnp.int32)
    earlier = (seq_ids[None, :] < seq_ids[:, None]) & (assign[None, :] == assign[:, None])
    offsets = jnp.sum(jnp.where(earlier, counts[None, :], 0), axis=1).astype(jnp.int32)
    return counts, starts, offsets, seq_ids


def reference(hidden, queries, key_weight, value_weight, lengths, assign):
    counts, starts, offsets, seq_ids = layout(lengths, assign)
    share = H // KVH

    def one_group(group_id):
        slot_ids = jnp.arange(SLOTS, dtype=jnp.int32)
        unit_ids = slot_ids // N_GRP
        lane_ids = slot_ids % N_GRP
        recv_hit = (assign[None, :] == group_id) & (offsets[None, :] <= unit_ids[:, None]) & (unit_ids[:, None] < offsets[None, :] + counts[None, :])
        slot_live = jnp.any(recv_hit, axis=1)
        source = jnp.sum(jnp.where(recv_hit, starts[None, :] + unit_ids[:, None] - offsets[None, :], 0), axis=1).astype(jnp.int32)
        slot_seq = jnp.where(slot_live, jnp.sum(jnp.where(recv_hit, seq_ids[None, :], 0), axis=1), -1).astype(jnp.int32)
        inner_pos = (jnp.sum(jnp.where(recv_hit, (unit_ids[:, None] - offsets[None, :]) * N_GRP, 0), axis=1) + lane_ids).astype(jnp.int32)
        seq_span = jnp.sum(jnp.where(recv_hit, counts[None, :] * N_GRP, 0), axis=1).astype(jnp.int32)
        row_data = hidden[source, lane_ids].reshape(SLOTS, N_SP, D)
        row_data = jnp.where(slot_live[:, None, None], row_data, jnp.zeros((), hidden.dtype))
        query_data = queries[source, lane_ids].reshape(SLOTS, N_SP, H, HD)
        flat_rows = jnp.transpose(row_data, (1, 0, 2)).reshape(N_SP * SLOTS, D)
        flat_query = jnp.transpose(query_data, (1, 0, 2, 3)).reshape(N_SP * SLOTS, H, HD)
        positions = (jnp.arange(N_SP, dtype=jnp.int32)[:, None] * seq_span[None, :] + inner_pos[None, :]).reshape(-1)
        row_seq = jnp.tile(slot_seq, N_SP)
        row_live = jnp.tile(slot_live, N_SP)
        key_sum = jnp.dot(flat_rows, key_weight, preferred_element_type=jnp.float32).reshape(-1, KVH, HD)
        key_rows = rotate(key_sum, positions).astype(jnp.bfloat16)
        values = jnp.dot(flat_rows, value_weight, preferred_element_type=jnp.float32).reshape(-1, KVH, HD).astype(jnp.bfloat16)
        allowed = (row_seq[:, None] == row_seq[None, :]) & row_live[:, None] & row_live[None, :] & (positions[None, :] <= positions[:, None])

        def one_head(head_id):
            kv_head = head_id // share
            head_keys = lax.dynamic_index_in_dim(key_rows, kv_head, 1, keepdims=False)
            head_values = lax.dynamic_index_in_dim(values, kv_head, 1, keepdims=False)
            head_query = lax.dynamic_index_in_dim(flat_query, head_id, 1, keepdims=False)
            scores = jnp.dot(head_query, head_keys.T, preferred_element_type=jnp.float32) * (HD ** -0.5)
            scores = jnp.where(allowed, scores, NEG_FILL)
            row_max = jnp.max(scores, axis=1, keepdims=True)
            weights = jnp.exp(scores - row_max)
            weights = (weights / jnp.sum(weights, axis=1, keepdims=True)).astype(jnp.bfloat16)
            result = jnp.dot(weights, head_values, preferred_element_type=jnp.float32)
            return jnp.where(row_live[:, None], result, 0.0).astype(jnp.bfloat16)

        per_head = lax.map(one_head, jnp.arange(H, dtype=jnp.int32))
        result = jnp.transpose(per_head, (1, 0, 2)).reshape(N_SP, SLOTS, H * HD)
        return jnp.transpose(result, (1, 0, 2)).reshape(SLOTS, N_SP * H * HD)

    return lax.map(one_group, jnp.arange(N_GRP, dtype=jnp.int32))
```

```python
import functools

import jax
import jax.numpy as jnp
from jax import lax
from jax.experimental import pallas as pl
from jax.experimental.pallas import tpu as pltpu
from jax.sharding import PartitionSpec as P

H = 16
KVH = 4
SHARE = H // KVH
HD = 128
ROPE_BASE = 500000.0
NEG_FILL = -1e30
LOG2E = 1.4426950408889634
MESH = pl.DeviceIdType.MESH
VMEM_BYTES = 56 * 1024 * 1024


def sequence_table(lengths, assign, groups, pieces):
    counts = lengths // (groups * pieces)
    starts = jnp.cumsum(counts) - counts
    seq_ids = jnp.arange(lengths.shape[0], dtype=jnp.int32)
    earlier = (seq_ids[None, :] < seq_ids[:, None]) & (assign[None, :] == assign[:, None])
    offsets = jnp.sum(jnp.where(earlier, counts[None, :], 0), axis=1)
    return counts, starts, offsets, seq_ids


def project_kernel(
    hid_ref, q_ref, wk_ref, wv_ref, sel_ref, cos_ref, sin_ref,
    kv_out, q_out,
    hid, w, acc, kvp, qp, rkv, rq,
    hid_sem, za_sem, zb_sem, xy_sem, kv_send, kv_recv, q_send, q_recv,
):
    groups = 32
    pieces = 16
    g = lax.axis_index("grp")
    z = lax.axis_index("sp")
    core = lax.rem(g, 2)
    chip = g // 2
    x = lax.rem(chip, 4)
    y = chip // 4
    zq = z // 4
    zm = lax.rem(z, 4)

    barrier = pltpu.get_barrier_semaphore()

    def greet(k, carry):
        peer = lax.rem(g + k, groups)
        pl.semaphore_signal(barrier, inc=1, device_id=(peer, z), device_id_type=MESH)
        return carry

    lax.fori_loop(1, groups, greet, 0)
    for step in (1, 2, 4, 8, 12, 14, 15):
        pl.semaphore_signal(
            barrier, inc=1, device_id=(g, lax.rem(z + step, pieces)), device_id_type=MESH
        )

    mine = jnp.where(
        core == 0,
        wk_ref[pl.ds(pl.multiple_of(chip * 16, 16), 16), :],
        wv_ref[pl.ds(pl.multiple_of(chip * 16, 16), 16), :],
    )
    w[zq, zm, y, x] = mine
    hid[core] = hid_ref[...]
    pl.semaphore_wait(barrier, groups - 1 + 7)

    hid_copy = pltpu.make_async_remote_copy(
        src_ref=hid.at[core], dst_ref=hid.at[core],
        send_sem=hid_sem.at[0], recv_sem=hid_sem.at[1],
        device_id=(g + 1 - 2 * core, z), device_id_type=MESH,
    )

    za = []
    for k in range(3):
        za.append(
            pltpu.make_async_remote_copy(
                src_ref=w.at[zq, zm, y, x], dst_ref=w.at[zq, zm, y, x],
                send_sem=za_sem.at[0, k], recv_sem=za_sem.at[1, k],
                device_id=(g, lax.rem(z + 4 * (k + 1), pieces)), device_id_type=MESH,
            )
        )
        za[-1].start()
    hid_copy.start()

    half_cols = q_ref.shape[1] // 2
    rows = q_ref.shape[0]
    qp[...] = (
        jnp.dot(sel_ref[:, :rows], q_ref[:, :half_cols], preferred_element_type=jnp.float32)
        + jnp.dot(sel_ref[:, rows:], q_ref[:, half_cols:], preferred_element_type=jnp.float32)
    ).astype(qp.dtype).reshape(qp.shape)

    def q_copy(k):
        peer = lax.rem(g + k, groups)
        return pltpu.make_async_remote_copy(
            src_ref=qp.at[peer], dst_ref=rq.at[g],
            send_sem=q_send.at[k], recv_sem=q_recv.at[g],
            device_id=(peer, z), device_id_type=MESH,
        )

    def q_wait(k):
        source = lax.rem(g + groups - k, groups)
        return pltpu.make_async_remote_copy(
            src_ref=qp.at[source], dst_ref=rq.at[source],
            send_sem=q_send.at[k], recv_sem=q_recv.at[source],
            device_id=(source, z), device_id_type=MESH,
        )

    def kv_copy(k):
        peer = lax.rem(g + k, groups)
        return pltpu.make_async_remote_copy(
            src_ref=kvp.at[peer], dst_ref=rkv.at[chip, core],
            send_sem=kv_send.at[k], recv_sem=kv_recv.at[g],
            device_id=(peer, z), device_id_type=MESH,
        )

    def kv_wait(k):
        source = lax.rem(g + groups - k, groups)
        return pltpu.make_async_remote_copy(
            src_ref=kvp.at[source], dst_ref=rkv.at[source // 2, lax.rem(source, 2)],
            send_sem=kv_send.at[k], recv_sem=kv_recv.at[source],
            device_id=(source, z), device_id_type=MESH,
        )

    for k in range(3):
        za[k].wait()
    zb = []
    for k, step in enumerate((1, 15, 2)):
        zb.append(
            pltpu.make_async_remote_copy(
                src_ref=w.at[:, zm, y, x], dst_ref=w.at[:, zm, y, x],
                send_sem=zb_sem.at[0, k], recv_sem=zb_sem.at[1, k],
                device_id=(g, lax.rem(z + step, pieces)), device_id_type=MESH,
            )
        )
        zb[-1].start()
    for k in range(3):
        zb[k].wait()

    lo = pl.ds(0, 256)
    hi = pl.ds(256, 256)

    def x_peer(step):
        return (2 * (y * 4 + lax.rem(x + step, 4)) + core, z)

    def y_peer(step):
        return (2 * (lax.rem(y + step, 4) * 4 + x) + core, z)

    def exchange(phase, plans):
        def copy(number, src, device, slot):
            return pltpu.make_async_remote_copy(
                src_ref=src, dst_ref=src,
                send_sem=xy_sem.at[phase, number, 0, slot],
                recv_sem=xy_sem.at[phase, number, 1, slot],
                device_id=device, device_id_type=MESH,
            )

        first = []
        for number, (place, view, peer) in enumerate(plans):
            up = copy(number, view(slice(None), place), peer(1), 0)
            down = copy(number, view(slice(None), place), peer(3), 1)
            up.start()
            down.start()
            first.append((up, down))
        second = []
        for number, (place, view, peer) in enumerate(plans):
            up, down = first[number]
            below = lax.rem(place + 3, 4)
            above = lax.rem(place + 1, 4)
            copy(number, view(slice(None), below), peer(3), 0).wait_recv()
            relay_up = copy(number, view(slice(0, 2), below), peer(1), 2)
            relay_up.start()
            copy(number, view(slice(None), above), peer(1), 1).wait_recv()
            relay_down = copy(number, view(slice(2, 4), above), peer(3), 3)
            relay_down.start()
            second.append((relay_up, relay_down))
        for number, (place, view, peer) in enumerate(plans):
            far = lax.rem(place + 2, 4)
            copy(number, view(slice(0, 2), far), peer(3), 2).wait_recv()
            copy(number, view(slice(2, 4), far), peer(1), 3).wait_recv()
            for each in first[number] + second[number]:
                each.wait_send()

    exchange(0, [
        (x, lambda q, n: w.at[q, :, y, n, :, lo], x_peer),
        (y, lambda q, n: w.at[q, :, n, x, :, hi], y_peer),
    ])
    lax.fori_loop(1, groups, lambda k, c: (q_copy(k).start(), c)[1], 0)
    exchange(1, [
        (y, lambda q, n: w.at[q, :, n, :, :, lo], y_peer),
        (x, lambda q, n: w.at[q, :, :, n, :, hi], x_peer),
    ])
    hid_copy.wait()

    acc[...] = jnp.zeros_like(acc)

    def project(s, carry):
        block = w[s // 4, lax.rem(s, 4)].reshape(256, 512)
        cols = pl.ds(pl.multiple_of(s * 256, 256), 256)
        for lane in range(2):
            acc[lane] += jnp.dot(hid[lane, :, cols], block, preferred_element_type=jnp.float32)
        return carry

    lax.fori_loop(0, pieces, project, 0)
    sel = sel_ref[...]
    cos = cos_ref[...]
    sin = sin_ref[...]
    for b in range(KVH):
        part = acc[:, :, b * HD : (b + 1) * HD].reshape(2 * rows, HD)
        turned = (part * cos + pltpu.roll(part, HD // 2, 1) * sin).astype(jnp.bfloat16)
        kvp[:, :, b * HD : (b + 1) * HD] = (
            jnp.dot(sel, turned, preferred_element_type=jnp.float32)
            .astype(jnp.bfloat16)
            .reshape(groups, 16, HD)
        )

    lax.fori_loop(1, groups, lambda k, c: (kv_copy(k).start(), c)[1], 0)
    rkv[chip, core] = kvp[g]
    rq[g] = qp[g]

    def unpack_q(half):
        slot = lax.broadcasted_iota(jnp.int32, (192, 512), 0)
        col = lax.broadcasted_iota(jnp.int32, (192, 512), 1)
        hit = (slot == (col & 7) * 32 + (col >> 4)) & (((col >> 3) & 1) == half)
        return hit.astype(jnp.float32).astype(jnp.bfloat16)

    lax.fori_loop(1, groups, lambda k, c: (q_wait(k).wait_recv(), c)[1], 0)
    arrived = rq[...].reshape(512, 1024)
    for half in range(2):
        dense = jnp.dot(unpack_q(half), arrived, preferred_element_type=jnp.float32)
        for h in range(8):
            q_out[half * 8 + h] = dense[:, h * HD : (h + 1) * HD].astype(q_out.dtype)

    slot = lax.broadcasted_iota(jnp.int32, (192, 256), 0)
    col = lax.broadcasted_iota(jnp.int32, (192, 256), 1)
    unpack = (slot == (col & 7) * 32 + (col >> 3)).astype(jnp.float32).astype(jnp.bfloat16)
    lax.fori_loop(1, groups, lambda k, c: (kv_wait(k).wait_recv(), c)[1], 0)
    for kind in range(2):
        dense = jnp.dot(
            unpack, rkv[:, kind].reshape(256, 512), preferred_element_type=jnp.float32
        )
        for b in range(KVH):
            kv_out[b, kind] = dense[:, b * HD : (b + 1) * HD].astype(kv_out.dtype)

    def finish(k, carry):
        q_copy(k).wait_send()
        kv_copy(k).wait_send()
        return carry

    lax.fori_loop(1, groups, finish, 0)


def ring_kernel(
    q_ref, kv_ref, bias_ref, live_ref, o_ref,
    buf, top, total, acc, send_sem, recv_sem,
):
    pieces = 16
    half = pieces // 2
    g = lax.axis_index("grp")
    me = lax.axis_index("sp")
    above = lax.rem(me + 1, pieces)
    below = lax.rem(me + pieces - 1, pieces)

    barrier = pltpu.get_barrier_semaphore()
    for peer in (above, below):
        pl.semaphore_signal(barrier, inc=1, device_id=(g, peer), device_id_type=MESH)
    pl.semaphore_wait(barrier, 2)

    def copy(way, step, b, first=False):
        if way == 0:
            piece = lax.rem(me - step + pieces, pieces)
            peer = above
        else:
            piece = lax.rem(me + step, pieces)
            peer = below
        src = kv_ref.at[b] if first else buf.at[piece, b]
        return pltpu.make_async_remote_copy(
            src_ref=src, dst_ref=buf.at[piece, b],
            send_sem=send_sem.at[way, step, b], recv_sem=recv_sem.at[way, step, b],
            device_id=(g, peer), device_id_type=MESH,
        )

    def arrival(way, step, b):
        if way == 0:
            piece = lax.rem(me - step - 1 + pieces, pieces)
            peer = below
        else:
            piece = lax.rem(me + step + 1, pieces)
            peer = above
        return pltpu.make_async_remote_copy(
            src_ref=buf.at[piece, b], dst_ref=buf.at[piece, b],
            send_sem=send_sem.at[way, step, b], recv_sem=recv_sem.at[way, step, b],
            device_id=(g, peer), device_id_type=MESH,
        )

    for b in range(KVH):
        copy(0, 0, b, True).start()
        copy(1, 0, b, True).start()

    scale = HD ** -0.5 * LOG2E

    def block(b, keys, values, bias, first):
        for h in range(SHARE):
            scores = (
                lax.dot_general(
                    q_ref[b * SHARE + h], keys, (((1,), (1,)), ((), ())),
                    preferred_element_type=jnp.float32,
                )
                * scale
                + bias
            )
            high = jnp.max(scores, axis=1, keepdims=True)
            if first:
                new_top = jnp.broadcast_to(high, (192, HD))
            else:
                old_top = top[b, h]
                new_top = jnp.maximum(old_top, high)
                fade = jnp.exp2(old_top - new_top)
            weights = jnp.exp2(scores - new_top[:, :1])
            part = jnp.dot(weights.astype(jnp.bfloat16), values, preferred_element_type=jnp.float32)
            added = jnp.sum(weights, axis=1, keepdims=True)
            if first:
                total[b, h] = jnp.broadcast_to(added, (192, HD))
                acc[b, h] = part
            else:
                total[b, h] = total[b, h] * fade + added
                acc[b, h] = acc[b, h] * fade + part
            top[b, h] = new_top

    def own(b, carry):
        block(b, kv_ref[b, 0], kv_ref[b, 1], bias_ref[1], True)
        return carry

    lax.fori_loop(0, KVH, own, 0)

    def attend(piece, b):
        block(b, buf[piece, b, 0], buf[piece, b, 1], bias_ref[0], False)

    def ring(index, carry):
        step = index // KVH
        b = lax.rem(index, KVH)
        arrival(0, step, b).wait_recv()

        @pl.when((step < half - 2) | (b < KVH // 2))
        def _():
            copy(0, step + 1, b).start()

        arrival(1, step, b).wait_recv()

        @pl.when((step < half - 2) | (b >= KVH // 2))
        def _():
            copy(1, step + 1, b).start()

        @pl.when(me - step - 1 >= 0)
        def _():
            attend(me - step - 1, b)

        @pl.when(me + step + 1 >= pieces)
        def _():
            attend(me + step + 1 - pieces, b)

        return carry

    lax.fori_loop(0, (half - 1) * KVH, ring, 0)

    for b in range(KVH):
        arrival(0 if b < KVH // 2 else 1, half - 1, b).wait_recv()

        @pl.when(me >= half)
        def _():
            attend(me - half, b)

    def emit(b, carry):
        for h in range(SHARE):
            cols = pl.ds(pl.multiple_of(b * (SHARE * HD), SHARE * HD) + h * HD, HD)
            o_ref[:, cols] = jnp.where(
                live_ref[...] > 0, acc[b, h] / total[b, h], 0.0
            ).astype(o_ref.dtype)
        return carry

    lax.fori_loop(0, KVH, emit, 0)

    for b in range(KVH):
        copy(0, 0, b, True).wait_send()
        copy(1, 0, b, True).wait_send()

    def finish(index, carry):
        step = index // KVH
        b = lax.rem(index, KVH)
        copy(0, step, b).wait_send()
        copy(1, step, b).wait_send()
        return carry

    lax.fori_loop(KVH, (half - 1) * KVH, finish, 0)
    for b in range(KVH):
        copy(0 if b < KVH // 2 else 1, half - 1, b).wait_send()


def per_device(hidden, queries, key_weight, value_weight, lengths, assign):
    groups = lax.axis_size("grp")
    pieces = lax.axis_size("sp")
    group_index = lax.axis_index("grp")
    piece_index = lax.axis_index("sp")
    rows = hidden.shape[0]
    capacity = 2 * (rows // groups) - 2
    slots = capacity * groups
    counts, starts, offsets, seq_ids = sequence_table(lengths, assign, groups, pieces)

    unit_send = jnp.arange(8, dtype=jnp.int32)[None, :, None]
    targets = jnp.arange(groups, dtype=jnp.int32)[:, None, None]
    send_hit = (assign == targets) & (offsets <= unit_send) & (unit_send < offsets + counts)
    send_row = jnp.sum(jnp.where(send_hit, starts + unit_send - offsets + 1, 0), axis=2) - 1
    source = (
        jnp.arange(2, dtype=jnp.int32)[None, :, None] * rows + send_row[:, None, :]
    )
    source = jnp.where(send_row[:, None, :] >= 0, source, -1).reshape(groups * 16, 1)
    sel = (source == jnp.arange(2 * rows, dtype=jnp.int32)[None, :]).astype(jnp.bfloat16)

    row_ids = jnp.arange(rows, dtype=jnp.int32)
    row_hit = (starts[None, :] <= row_ids[:, None]) & (row_ids[:, None] < (starts + counts)[None, :])
    base = jnp.sum(
        jnp.where(
            row_hit,
            piece_index * counts[None, :] * groups + (row_ids[:, None] - starts[None, :]) * groups,
            0,
        ),
        axis=1,
    )
    lanes = 2 * (group_index // 2) + jnp.arange(2, dtype=jnp.int32)
    positions = (base[None, :] + lanes[:, None]).reshape(-1)
    frequency = ROPE_BASE ** (-2.0 * jnp.arange(HD // 2, dtype=jnp.float32) / HD)
    angles = positions.astype(jnp.float32)[:, None] * frequency[None, :]
    is_key = group_index % 2 == 0
    cos = jnp.where(is_key, jnp.cos(angles), 1.0)
    sin = jnp.where(is_key, jnp.sin(angles), 0.0)
    cos = jnp.concatenate([cos, cos], axis=1)
    sin = jnp.concatenate([-sin, sin], axis=1)

    slot_ids = jnp.arange(slots, dtype=jnp.int32)
    unit_ids = slot_ids // groups
    recv_hit = (
        (assign[None, :] == group_index)
        & (offsets[None, :] <= unit_ids[:, None])
        & (unit_ids[:, None] < offsets[None, :] + counts[None, :])
    )
    slot_live = jnp.any(recv_hit, axis=1)
    slot_seq = jnp.where(slot_live, jnp.sum(jnp.where(recv_hit, seq_ids[None, :], 0), axis=1), -1)
    same = (slot_seq[:, None] == slot_seq[None, :]) & slot_live[:, None] & slot_live[None, :]
    causal = same & (slot_ids[None, :] <= slot_ids[:, None])
    bias = jnp.where(jnp.stack([same, causal]), 0.0, NEG_FILL).astype(jnp.float32)
    live = jnp.broadcast_to(slot_live[:, None].astype(jnp.float32), (slots, HD))

    vmem = pl.BlockSpec(memory_space=pltpu.VMEM)
    bf16 = jnp.bfloat16
    dma = pltpu.SemaphoreType.DMA
    kv, q = pl.pallas_call(
        project_kernel,
        out_shape=(
            jax.ShapeDtypeStruct((KVH, 2, slots, HD), bf16),
            jax.ShapeDtypeStruct((H, slots, HD), bf16),
        ),
        in_specs=[vmem] * 7,
        out_specs=(vmem, vmem),
        scratch_shapes=[
            pltpu.VMEM((2, rows, 4096), bf16),
            pltpu.VMEM((4, 4, 4, 4, 16, 512), bf16),
            pltpu.VMEM((2, rows, 512), jnp.float32),
            pltpu.VMEM((groups, 16, 512), bf16),
            pltpu.VMEM((groups, 16, 1024), bf16),
            pltpu.VMEM((groups // 2, 2, 16, 512), bf16),
            pltpu.VMEM((groups, 16, 1024), bf16),
            dma((2,)),
            dma((2, 3)),
            dma((2, 3)),
            dma((2, 2, 2, 4)),
            dma((groups,)),
            dma((groups,)),
            dma((groups,)),
            dma((groups,)),
        ],
        compiler_params=pltpu.CompilerParams(
            collective_id=0, has_side_effects=True, vmem_limit_bytes=VMEM_BYTES
        ),
        name="project",
    )(
        hidden.reshape(rows, -1), queries.reshape(rows, -1), key_weight, value_weight, sel, cos, sin
    )

    out = pl.pallas_call(
        ring_kernel,
        out_shape=jax.ShapeDtypeStruct((slots, H * HD), bf16),
        in_specs=[vmem] * 4,
        out_specs=vmem,
        scratch_shapes=[
            pltpu.VMEM((pieces, KVH, 2, slots, HD), bf16),
            pltpu.VMEM((KVH, SHARE, slots, HD), jnp.float32),
            pltpu.VMEM((KVH, SHARE, slots, HD), jnp.float32),
            pltpu.VMEM((KVH, SHARE, slots, HD), jnp.float32),
            dma((2, pieces // 2, KVH)),
            dma((2, pieces // 2, KVH)),
        ],
        compiler_params=pltpu.CompilerParams(
            collective_id=1, has_side_effects=True, vmem_limit_bytes=VMEM_BYTES
        ),
        name="ring",
    )(q, kv, bias, live)
    return out.reshape(1, slots, H * HD)


def solution(mesh):
    return jax.shard_map(
        per_device,
        mesh=mesh,
        in_specs=(
            P(None, "grp", "sp"),
            P(None, "grp", "sp"),
            P("sp", None),
            P("sp", None),
            P(),
            P(),
        ),
        out_specs=P("grp", None, "sp"),
        check_vma=False,
    )
```

```python
import jax
import jax.numpy as jnp
from jax import lax
from jax.experimental import pallas as pl
from jax.experimental.pallas import tpu as pltpu
from jax.sharding import PartitionSpec as P

H = 16
KVH = 4
SHARE = H // KVH
HD = 128
GROUPS = 32
PIECES = 16
ROWS = 128
SLOTS = 192
HALF = PIECES // 2
PAIR = KVH // 2
COLS = PAIR * HD
ROPE_BASE = 500000.0
NEG_FILL = -1e30
LOG2E = 1.4426950408889634
MESH = pl.DeviceIdType.MESH
VMEM_BYTES = 56 * 1024 * 1024
F32 = jnp.float32
BF16 = jnp.bfloat16


def iota(shape, dim):
    return lax.broadcasted_iota(jnp.int32, shape, dim)


def kernel(
    hid_ref, q_ref, wk_ref, wv_ref, len_row, len_col, asg_row, asg_col, freq_ref,
    o_ref, live_ref,
    hid, qin, w, acc, sel, cos, sin, kvp, qp, rkv, rq, qd, buf, bias, top, total, out_acc,
    in_sem, hid_sem, za_sem, zb_sem, xa_sem, xb_sem,
    kv_send, kv_recv, q_send, q_recv, ring_send, ring_recv,
):
    g = lax.axis_index("grp")
    z = lax.axis_index("sp")
    core = lax.rem(g, 2)
    chip = g // 2
    x = lax.rem(chip, 4)
    y = chip // 4
    zq = z // 4
    zm = lax.rem(z, 4)

    barrier = pltpu.get_barrier_semaphore()

    def greet(k, carry):
        peer = lax.rem(g + k, GROUPS)
        pl.semaphore_signal(barrier, inc=1, device_id=(peer, z), device_id_type=MESH)
        return carry

    lax.fori_loop(1, GROUPS, greet, 0)
    for step in (1, 2, 4, 8, 12, 14, 15):
        pl.semaphore_signal(
            barrier, inc=1, device_id=(g, lax.rem(z + step, PIECES)), device_id_type=MESH
        )

    hid_in = pltpu.make_async_copy(hid_ref, hid.at[core], in_sem.at[0])
    q_in = pltpu.make_async_copy(q_ref, qin, in_sem.at[1])
    hid_in.start()
    q_in.start()
    own_rows = pl.ds(pl.multiple_of(chip * 16, 16), 16)
    w[zq, zm, y, x] = jnp.where(core == 0, wk_ref[own_rows, :], wv_ref[own_rows, :])

    counts_r = (len_row[...] // (GROUPS * PIECES)).astype(F32)
    counts_c = (len_col[...] // (GROUPS * PIECES)).astype(F32)
    asg_r = asg_row[...]
    asg_c = asg_col[...]
    nseq = counts_r.shape[1]
    first = iota((nseq, nseq), 0)
    second = iota((nseq, nseq), 1)
    same_group = asg_c == asg_r
    up_c = jnp.where(first < second, counts_c, 0.0)
    up_r = jnp.where(second < first, counts_r, 0.0)
    starts_r = jnp.sum(up_c, axis=0, keepdims=True)
    starts_c = jnp.sum(up_r, axis=1, keepdims=True)
    offsets_r = jnp.sum(jnp.where(same_group, up_c, 0.0), axis=0, keepdims=True)
    offsets_c = jnp.sum(jnp.where(same_group, up_r, 0.0), axis=1, keepdims=True)

    pl.semaphore_wait(barrier, GROUPS - 1 + 7)

    def cols(half):
        return pl.ds(half * COLS, COLS)

    def rdma(src, dst, send, recv, device):
        return pltpu.make_async_remote_copy(
            src_ref=src, dst_ref=dst, send_sem=send, recv_sem=recv,
            device_id=device, device_id_type=MESH,
        )

    def za(half, k):
        part = w.at[zq, zm, y, x, :, cols(half)]
        return rdma(
            part, part, za_sem.at[half, 0, k], za_sem.at[half, 1, k],
            (g, lax.rem(z + 4 * (k + 1), PIECES)),
        )

    def zb(half, k):
        part = w.at[:, zm, y, x, :, cols(half)]
        return rdma(
            part, part, zb_sem.at[half, 0, k], zb_sem.at[half, 1, k],
            (g, lax.rem(z + (1, 15, 2)[k], PIECES)),
        )

    def x_peer(step):
        return (2 * (y * 4 + lax.rem(x + step, 4)) + core, z)

    def y_peer(step):
        return (2 * (lax.rem(y + step, 4) * 4 + x) + core, z)

    def xa(half, path, k):
        if path == 0:
            part = w.at[0:2, :, y, x, :, cols(half)]
        else:
            part = w.at[2:4, :, y, x, :, cols(half)]
        return rdma(
            part, part, xa_sem.at[half, path, 0, k], xa_sem.at[half, path, 1, k],
            (x_peer, y_peer)[path](k + 1),
        )

    def xb_view(half, path, shards, place):
        if path == 0:
            return w.at[shards, :, place, :, :, cols(half)]
        return w.at[shards, :, :, place, :, cols(half)]

    def xb(half, path, kind):
        place = (y, x)[path]
        peer = (y_peer, x_peer)[path]
        low = 2 * path
        if kind == 0:
            src, device = xb_view(half, path, slice(low, low + 2), place), peer(1)
        elif kind == 1:
            src, device = xb_view(half, path, slice(low, low + 2), place), peer(3)
        elif kind == 2:
            src, device = xb_view(half, path, slice(low, low + 1), lax.rem(place + 3, 4)), peer(1)
        else:
            src, device = (
                xb_view(half, path, slice(low + 1, low + 2), lax.rem(place + 1, 4)), peer(3)
            )
        return rdma(
            src, src, xb_sem.at[half, path, 0, kind], xb_sem.at[half, path, 1, kind], device
        )

    def xb_start(half):
        for path in range(2):
            xb(half, path, 0).start()
            xb(half, path, 1).start()

    def xb_relay(half):
        for path in range(2):
            xb(half, path, 0).wait_recv()
            xb(half, path, 2).start()
            xb(half, path, 1).wait_recv()
            xb(half, path, 3).start()

    def xb_finish(half):
        for path in range(2):
            xb(half, path, 2).wait_recv()
            xb(half, path, 3).wait_recv()

    for half in range(2):
        for k in range(3):
            za(half, k).start()
    hid_in.wait()
    hid_copy = rdma(
        hid.at[core], hid.at[core], hid_sem.at[0], hid_sem.at[1], (g + 1 - 2 * core, z)
    )
    hid_copy.start()

    row_l = iota((nseq, ROWS), 1).astype(F32)
    here = (starts_c <= row_l) & (row_l < starts_c + counts_c)
    goal = jnp.sum(
        jnp.where(here, asg_c.astype(F32) * 16.0 + offsets_c + row_l - starts_c, 0.0),
        axis=0, keepdims=True,
    ).astype(jnp.int32)
    goal = jnp.concatenate([goal, goal + 8], axis=1)
    sel[...] = (iota((GROUPS * 16, 2 * ROWS), 0) == goal).astype(F32).astype(BF16)

    def w_z():
        for half in range(2):
            for k in range(3):
                za(half, k).wait_recv()
            for k in range(3):
                zb(half, k).start()

    w_z()
    row_s = iota((ROWS, nseq), 0).astype(F32)
    here = (starts_r <= row_s) & (row_s < starts_r + counts_r)
    base = jnp.sum(
        jnp.where(
            here,
            z.astype(F32) * counts_r * GROUPS + (row_s - starts_r) * GROUPS,
            0.0,
        ),
        axis=1, keepdims=True,
    )
    is_key = core == 0
    for lane in range(2):
        angles = (base + (2 * chip + lane).astype(F32)) * freq_ref[...]
        cosine = jnp.where(is_key, jnp.cos(angles), 1.0)
        sine = jnp.where(is_key, jnp.sin(angles), 0.0)
        at = pl.ds(lane * ROWS, ROWS)
        cos[at, :] = cosine
        sin[at, :] = jnp.where(iota((ROWS, HD), 1) < HD // 2, -sine, sine)

    for k in range(3):
        zb(0, k).wait_recv()
    for path in range(2):
        for k in range(3):
            xa(0, path, k).start()

    q_in.wait()
    q_cols = H * HD // 2
    qp[...] = (
        jnp.dot(sel[:, :ROWS], qin[:, :q_cols], preferred_element_type=F32)
        + jnp.dot(sel[:, ROWS:], qin[:, q_cols:], preferred_element_type=F32)
    ).astype(BF16).reshape(qp.shape)

    for k in range(3):
        zb(1, k).wait_recv()
    for path in range(2):
        for k in range(3):
            xa(0, path, k).wait_recv()
    xb_start(0)
    xb_relay(0)
    xb_finish(0)
    for path in range(2):
        for k in range(3):
            xa(1, path, k).start()
    hid_copy.wait_recv()

    def project(half):
        acc[...] = jnp.zeros_like(acc)

        def shard(s, carry):
            block = w[s // 4, lax.rem(s, 4), :, :, :, cols(half)].reshape(256, COLS)
            part = pl.ds(pl.multiple_of(s * 256, 256), 256)
            for lane in range(2):
                acc[lane] += jnp.dot(hid[lane, :, part], block, preferred_element_type=F32)
            return carry

        lax.fori_loop(0, PIECES, shard, 0)
        for b in range(PAIR):
            at = pl.ds(b * HD, HD)
            part = acc[:, :, at].reshape(2 * ROWS, HD)
            turned = (part * cos[...] + pltpu.roll(part, HD // 2, 1) * sin[...]).astype(BF16)
            kvp[half, :, :, at] = (
                jnp.dot(sel[...], turned, preferred_element_type=F32)
                .astype(BF16)
                .reshape(GROUPS, 16, HD)
            )

    def kv_copy(half, k):
        peer = lax.rem(g + k, GROUPS)
        return rdma(
            kvp.at[half, peer], rkv.at[half, chip, core],
            kv_send.at[half, k], kv_recv.at[half, g], (peer, z),
        )

    def kv_wait(half, k):
        source = lax.rem(g + GROUPS - k, GROUPS)
        return rdma(
            kvp.at[half, source], rkv.at[half, source // 2, lax.rem(source, 2)],
            kv_send.at[half, k], kv_recv.at[half, source], (source, z),
        )

    def q_copy(k):
        peer = lax.rem(g + k, GROUPS)
        return rdma(qp.at[peer], rq.at[g], q_send.at[k], q_recv.at[g], (peer, z))

    def q_wait(k):
        source = lax.rem(g + GROUPS - k, GROUPS)
        return rdma(
            qp.at[source], rq.at[source], q_send.at[k], q_recv.at[source], (source, z)
        )

    def each_peer(act):
        def body(k, carry):
            act(k)
            return carry

        lax.fori_loop(1, GROUPS, body, 0)

    def kv_begin(half):
        each_peer(lambda k: kv_copy(half, k).start())
        rkv[half, chip, core] = kvp[half, g]

    def kv_end(half):
        slot = iota((SLOTS, 256), 0)
        col = iota((SLOTS, 256), 1)
        unpack = (slot == (col & 7) * GROUPS + (col >> 3)).astype(F32).astype(BF16)
        each_peer(lambda k: kv_wait(half, k).wait_recv())
        for kind in range(2):
            dense = jnp.dot(
                unpack, rkv[half, :, kind].reshape(256, COLS), preferred_element_type=F32
            )
            for b in range(PAIR):
                buf[z, half * PAIR + b, kind] = dense[:, b * HD : (b + 1) * HD].astype(BF16)

    above = lax.rem(z + 1, PIECES)
    below = lax.rem(z + PIECES - 1, PIECES)

    def ring_copy(way, step, b):
        if way == 0:
            piece, peer = lax.rem(z - step + PIECES, PIECES), above
        else:
            piece, peer = lax.rem(z + step, PIECES), below
        return rdma(
            buf.at[piece, b], buf.at[piece, b],
            ring_send.at[way, step, b], ring_recv.at[way, step, b], (g, peer),
        )

    def arrival(way, step, b):
        if way == 0:
            piece, peer = lax.rem(z - step - 1 + PIECES, PIECES), below
        else:
            piece, peer = lax.rem(z + step + 1, PIECES), above
        return rdma(
            buf.at[piece, b], buf.at[piece, b],
            ring_send.at[way, step, b], ring_recv.at[way, step, b], (g, peer),
        )

    def ring_begin(half):
        for b in range(half * PAIR, half * PAIR + PAIR):
            ring_copy(0, 0, b).start()
            ring_copy(1, 0, b).start()

    def relay(step, b):
        last = step >= HALF - 2
        first_head = lax.rem(b, PAIR) == 0
        arrival(0, step, b).wait_recv()

        @pl.when(jnp.logical_not(last) | first_head)
        def _():
            ring_copy(0, step + 1, b).start()

        arrival(1, step, b).wait_recv()

        @pl.when(jnp.logical_not(last) | jnp.logical_not(first_head))
        def _():
            ring_copy(1, step + 1, b).start()

    scale = HD ** -0.5 * LOG2E

    def block(piece, b, first):
        keys = buf[piece, b, 0]
        values = buf[piece, b, 1]
        mask = bias[1 if first else 0]
        for h in range(SHARE):
            scores = (
                lax.dot_general(
                    qd[b * SHARE + h], keys, (((1,), (1,)), ((), ())), preferred_element_type=F32
                )
                * scale
                + mask
            )
            high = jnp.max(scores, axis=1, keepdims=True)
            if first:
                new_top = jnp.broadcast_to(high, (SLOTS, HD))
            else:
                old_top = top[b, h]
                new_top = jnp.maximum(old_top, high)
                fade = jnp.exp2(old_top - new_top)
            weights = jnp.exp2(scores - new_top[:, :1])
            part = jnp.dot(weights.astype(BF16), values, preferred_element_type=F32)
            added = jnp.sum(weights, axis=1, keepdims=True)
            if first:
                total[b, h] = jnp.broadcast_to(added, (SLOTS, HD))
                out_acc[b, h] = part
            else:
                total[b, h] = total[b, h] * fade + added
                out_acc[b, h] = out_acc[b, h] * fade + part
            top[b, h] = new_top

    def attend(step, b):
        @pl.when(z - step - 1 >= 0)
        def _():
            block(z - step - 1, b, False)

        @pl.when(z + step + 1 >= PIECES)
        def _():
            block(z + step + 1 - PIECES, b, False)

    def heads(half, act):
        def body(b, carry):
            act(b)
            return carry

        lax.fori_loop(half * PAIR, half * PAIR + PAIR, body, 0)

    def ring_last(half):
        for b in range(half * PAIR, half * PAIR + PAIR):
            arrival(b - half * PAIR, HALF - 1, b).wait_recv()

            @pl.when(z >= HALF)
            def _():
                block(z - HALF, b, False)

    def emit(b):
        for h in range(SHARE):
            at = pl.ds(pl.multiple_of(b * (SHARE * HD), SHARE * HD) + h * HD, HD)
            o_ref[:, at] = (out_acc[b, h] / total[b, h]).astype(BF16)

    project(0)
    kv_begin(0)
    each_peer(lambda k: q_copy(k).start())
    rq[g] = qp[g]
    for path in range(2):
        for k in range(3):
            xa(1, path, k).wait_recv()
    kv_end(0)
    ring_begin(0)
    xb_start(1)

    unit_s = (iota((SLOTS, nseq), 0) >> 5).astype(F32)
    hit = (asg_r == g) & (offsets_r <= unit_s) & (unit_s < offsets_r + counts_r)
    seq_s = jnp.sum(jnp.where(hit, iota((SLOTS, nseq), 1) + 1, 0).astype(F32), axis=1, keepdims=True)
    unit_l = (iota((nseq, SLOTS), 1) >> 5).astype(F32)
    hit = (asg_c == g) & (offsets_c <= unit_l) & (unit_l < offsets_c + counts_c)
    seq_l = jnp.sum(jnp.where(hit, iota((nseq, SLOTS), 0) + 1, 0).astype(F32), axis=0, keepdims=True)
    same = (seq_s == seq_l) & (seq_s > 0.5)
    bias[0] = jnp.where(same, 0.0, NEG_FILL)
    bias[1] = jnp.where(
        same & (iota((SLOTS, SLOTS), 1) <= iota((SLOTS, SLOTS), 0)), 0.0, NEG_FILL
    )
    live_ref[...] = jnp.broadcast_to(seq_s, (SLOTS, HD))

    heads(0, lambda b: relay(0, b))
    heads(0, lambda b: relay(1, b))
    xb_relay(1)
    heads(0, lambda b: relay(2, b))

    each_peer(lambda k: q_wait(k).wait_recv())
    arrived = rq[...].reshape(GROUPS * 16, q_cols)
    slot = iota((SLOTS, GROUPS * 16), 0)
    col = iota((SLOTS, GROUPS * 16), 1)
    for part in range(2):
        unpack = (slot == (col & 7) * GROUPS + (col >> 4)) & (((col >> 3) & 1) == part)
        dense = jnp.dot(unpack.astype(F32).astype(BF16), arrived, preferred_element_type=F32)
        for h in range(H // 2):
            qd[part * (H // 2) + h] = dense[:, h * HD : (h + 1) * HD].astype(BF16)

    heads(0, lambda b: relay(3, b))
    heads(0, lambda b: block(z, b, True))

    def late(step):
        def act(b):
            relay(step, b)
            attend(step - 4, b)
            attend(step, b)

        return act

    xb_finish(1)
    project(1)
    kv_begin(1)
    heads(0, late(4))
    kv_end(1)
    ring_begin(1)
    heads(0, late(5))
    heads(1, lambda b: block(z, b, True))
    heads(0, late(6))

    def prompt(step, b):
        relay(step, b)
        attend(step, b)

    heads(1, lambda b: prompt(0, b))
    heads(0, lambda b: attend(3, b))
    heads(1, lambda b: prompt(1, b))
    ring_last(0)
    heads(0, emit)

    def steps(index, carry):
        prompt(index // PAIR, PAIR + lax.rem(index, PAIR))
        return carry

    lax.fori_loop(2 * PAIR, (HALF - 1) * PAIR, steps, 0)
    ring_last(1)
    heads(1, emit)

    hid_copy.wait_send()
    for half in range(2):
        for k in range(3):
            za(half, k).wait_send()
            zb(half, k).wait_send()
        for path in range(2):
            for k in range(3):
                xa(half, path, k).wait_send()
            for kind in range(4):
                xb(half, path, kind).wait_send()
        each_peer(lambda k: kv_copy(half, k).wait_send())
    each_peer(lambda k: q_copy(k).wait_send())

    def ring_sent(index, carry):
        ring_copy(0, index // KVH, lax.rem(index, KVH)).wait_send()
        ring_copy(1, index // KVH, lax.rem(index, KVH)).wait_send()
        return carry

    lax.fori_loop(0, (HALF - 1) * KVH, ring_sent, 0)
    for b in range(KVH):
        ring_copy(b % PAIR, HALF - 1, b).wait_send()


def per_device(hidden, queries, key_weight, value_weight, lengths, assign):
    frequency = ROPE_BASE ** (-2.0 * jnp.arange(HD // 2, dtype=F32) / HD)
    frequency = jnp.concatenate([frequency, frequency]).reshape(1, HD)
    vmem = pl.BlockSpec(memory_space=pltpu.VMEM)
    hbm = pl.BlockSpec(memory_space=pl.ANY)
    dma = pltpu.SemaphoreType.DMA
    state = pltpu.VMEM((KVH, SHARE, SLOTS, HD), F32)
    out, live = pl.pallas_call(
        kernel,
        out_shape=(
            jax.ShapeDtypeStruct((SLOTS, H * HD), BF16),
            jax.ShapeDtypeStruct((SLOTS, HD), F32),
        ),
        in_specs=[hbm, hbm] + [vmem] * 7,
        out_specs=(vmem, vmem),
        scratch_shapes=[
            pltpu.VMEM((2, ROWS, 4096), BF16),
            pltpu.VMEM((ROWS, H * HD), BF16),
            pltpu.VMEM((4, 4, 4, 4, 16, 512), BF16),
            pltpu.VMEM((2, ROWS, COLS), F32),
            pltpu.VMEM((GROUPS * 16, 2 * ROWS), BF16),
            pltpu.VMEM((2 * ROWS, HD), F32),
            pltpu.VMEM((2 * ROWS, HD), F32),
            pltpu.VMEM((2, GROUPS, 16, COLS), BF16),
            pltpu.VMEM((GROUPS, 16, H * HD // 2), BF16),
            pltpu.VMEM((2, GROUPS // 2, 2, 16, COLS), BF16),
            pltpu.VMEM((GROUPS, 16, H * HD // 2), BF16),
            pltpu.VMEM((H, SLOTS, HD), BF16),
            pltpu.VMEM((PIECES, KVH, 2, SLOTS, HD), BF16),
            pltpu.VMEM((2, SLOTS, SLOTS), F32),
            state,
            state,
            state,
            dma((2,)),
            dma((2,)),
            dma((2, 2, 3)),
            dma((2, 2, 3)),
            dma((2, 2, 2, 3)),
            dma((2, 2, 2, 4)),
            dma((2, GROUPS)),
            dma((2, GROUPS)),
            dma((GROUPS,)),
            dma((GROUPS,)),
            dma((2, HALF, KVH)),
            dma((2, HALF, KVH)),
        ],
        compiler_params=pltpu.CompilerParams(
            collective_id=0, has_side_effects=True, vmem_limit_bytes=VMEM_BYTES
        ),
        name="attend",
    )(
        hidden.reshape(ROWS, -1),
        queries.reshape(ROWS, -1),
        key_weight,
        value_weight,
        lengths.reshape(1, -1),
        lengths.reshape(-1, 1),
        assign.reshape(1, -1),
        assign.reshape(-1, 1),
        frequency,
    )
    return jnp.where(live[:, :1] > 0.5, out, jnp.zeros((), BF16))[None]


def solution(mesh):
    return jax.shard_map(
        per_device,
        mesh=mesh,
        in_specs=(
            P(None, "grp", "sp"),
            P(None, "grp", "sp"),
            P("sp", None),
            P("sp", None),
            P(),
            P(),
        ),
        out_specs=P("grp", None, "sp"),
        check_vma=False,
    )
```

```python
import jax
import jax.numpy as jnp
import numpy as np
from jax import lax
from jax.experimental import pallas as pl
from jax.experimental.pallas import tpu as pltpu
from jax.sharding import PartitionSpec as P

H = 16
KVH = 4
SHARE = H // KVH
HD = 128
GROUPS = 32
PIECES = 16
ROWS = 128
SLOTS = 192
HALF = PIECES // 2
WIDE = SHARE * SLOTS
FIRST = 1
ROPE_BASE = 500000.0
NEG_FILL = -1e30
LOG2E = 1.4426950408889634
MESH = pl.DeviceIdType.MESH
VMEM_BYTES = 56 * 1024 * 1024
F32 = jnp.float32
BF16 = jnp.bfloat16


def iota(shape, dim):
    return lax.broadcasted_iota(jnp.int32, shape, dim)


def kernel(
    hid_ref, q_ref, wk_ref, wv_ref, len_ref, asg_ref, freq_ref,
    o_ref,
    hid, qin, w, sel, cos, sin, kvp, qp, rkv, rq, qd, buf, bias, live, top, total, out_acc,
    in_sem, hid_sem, wz_sem, xa_sem, xb_sem,
    kv_sem, q_sem, ring_send, ring_recv,
):
    g = lax.axis_index("grp")
    z = lax.axis_index("sp")
    core = lax.rem(g, 2)
    chip = g // 2
    x = lax.rem(chip, 4)
    y = chip // 4
    zq = z // 4
    zm = lax.rem(z, 4)

    def loop(low, high, act):
        def body(k, carry):
            act(k)
            return carry

        lax.fori_loop(low, high, body, 0)

    barrier = pltpu.get_barrier_semaphore()

    def greet(device):
        pl.semaphore_signal(barrier, inc=1, device_id=device, device_id_type=MESH)

    loop(1, PIECES, lambda k: greet((g, lax.rem(z + k, PIECES))))
    loop(1, GROUPS, lambda k: greet((lax.rem(g + k, GROUPS), z)))

    hid_in = pltpu.make_async_copy(hid_ref, hid.at[core], in_sem.at[0])
    q_in = pltpu.make_async_copy(q_ref, qin, in_sem.at[1])
    hid_in.start()
    q_in.start()
    own_rows = pl.ds(pl.multiple_of(chip * 16, 16), 16)
    w[zq, zm, y, x] = jnp.where(core == 0, wk_ref[own_rows, :], wv_ref[own_rows, :])

    nseq = len_ref.shape[1]
    first = iota((nseq, nseq), 0)
    second = iota((nseq, nseq), 1)
    diagonal = first == second
    counts_r = (len_ref[...] // (GROUPS * PIECES)).astype(F32)
    asg_r = asg_ref[...].astype(F32)
    counts_c = jnp.sum(jnp.where(diagonal, counts_r, 0.0), axis=1, keepdims=True)
    asg_c = jnp.sum(jnp.where(diagonal, asg_r, 0.0), axis=1, keepdims=True)
    same_group = asg_c == asg_r
    up_c = jnp.where(first < second, counts_c, 0.0)
    up_r = jnp.where(second < first, counts_r, 0.0)
    starts_r = jnp.sum(up_c, axis=0, keepdims=True)
    starts_c = jnp.sum(up_r, axis=1, keepdims=True)
    offsets_r = jnp.sum(jnp.where(same_group, up_c, 0.0), axis=0, keepdims=True)
    offsets_c = jnp.sum(jnp.where(same_group, up_r, 0.0), axis=1, keepdims=True)

    pl.semaphore_wait(barrier, GROUPS - 1 + PIECES - 1)

    def heads_of(part):
        return (0, FIRST) if part == 0 else (FIRST, KVH)

    def cols(part):
        low, high = heads_of(part)
        return pl.ds(low * HD, (high - low) * HD)

    def rdma(src, dst, send, recv, device):
        return pltpu.make_async_remote_copy(
            src_ref=src, dst_ref=dst, send_sem=send, recv_sem=recv,
            device_id=device, device_id_type=MESH,
        )

    def wz(part, step):
        slab = w.at[zq, zm, y, x, :, cols(part)]
        return rdma(
            slab, slab, wz_sem.at[part, 0], wz_sem.at[part, 1],
            (g, lax.rem(z + step, PIECES)),
        )

    def take(ref, sem):
        pltpu.make_async_copy(ref, ref, sem).wait()

    def wz_take(part, way):
        take(kvp.at[0 : PIECES - 1, :, cols(part)], wz_sem.at[part, way])

    def x_peer(step):
        return (2 * (y * 4 + lax.rem(x + step, 4)) + core, z)

    def y_peer(step):
        return (2 * (lax.rem(y + step, 4) * 4 + x) + core, z)

    def xa(part, path, k):
        slab = w.at[2 * path : 2 * path + 2, :, y, x, :, cols(part)]
        return rdma(
            slab, slab, xa_sem.at[part, path, 0, k], xa_sem.at[part, path, 1, k],
            (x_peer, y_peer)[path]((2, 1, 3)[k]),
        )

    def xb_view(part, path, shards, place):
        if path == 0:
            return w.at[shards, :, place, :, :, cols(part)]
        return w.at[shards, :, :, place, :, cols(part)]

    def xb(part, path, kind):
        place = (y, x)[path]
        peer = (y_peer, x_peer)[path]
        low = 2 * path
        both, one, two = slice(low, low + 2), slice(low, low + 1), slice(low + 1, low + 2)
        if part == 0:
            slab, device = xb_view(part, path, both, place), peer((2, 1, 3)[kind])
        else:
            slab, device = (
                (xb_view(part, path, one, place), peer(1)),
                (xb_view(part, path, two, place), peer(3)),
                (xb_view(part, path, two, place), peer(1)),
                (xb_view(part, path, one, place), peer(3)),
                (xb_view(part, path, one, lax.rem(place + 3, 4)), peer(1)),
                (xb_view(part, path, two, lax.rem(place + 1, 4)), peer(3)),
            )[kind]
        return rdma(
            slab, slab, xb_sem.at[part, path, 0, kind], xb_sem.at[part, path, 1, kind], device
        )

    def xb_start(kinds, part):
        for path in range(2):
            for kind in kinds:
                xb(part, path, kind).start()

    def xb_wait(kinds, part):
        for path in range(2):
            for kind in kinds:
                xb(part, path, kind).wait_recv()

    def xa_start(part):
        for path in range(2):
            for k in range(3):
                xa(part, path, k).start()

    def xa_wait(part):
        for path in range(2):
            for k in range(3):
                xa(part, path, k).wait_recv()

    for part in range(2):
        for step in (8, 7, 9, 6, 10, 5, 11, 4, 12, 3, 13, 2, 14, 1, 15):
            wz(part, step).start()
    hid_in.wait()
    hid_copy = rdma(
        hid.at[core], hid.at[core], hid_sem.at[0], hid_sem.at[1], (g + 1 - 2 * core, z)
    )
    hid_copy.start()

    row_l = iota((nseq, ROWS), 1).astype(F32)
    here = (starts_c <= row_l) & (row_l < starts_c + counts_c)
    goal = jnp.sum(
        jnp.where(here, asg_c * 16.0 + offsets_c + row_l - starts_c, 0.0), axis=0, keepdims=True
    ).astype(jnp.int32)
    goal = jnp.concatenate([goal, goal + 8], axis=1)
    sel[...] = (iota((GROUPS * 16, 2 * ROWS), 0) == goal).astype(F32).astype(BF16)

    wz_take(0, 1)
    xa_start(0)
    row_s = iota((ROWS, nseq), 0).astype(F32)
    here = (starts_r <= row_s) & (row_s < starts_r + counts_r)
    base = jnp.sum(
        jnp.where(
            here,
            z.astype(F32) * counts_r * GROUPS + (row_s - starts_r) * GROUPS,
            0.0,
        ),
        axis=1, keepdims=True,
    )
    is_key = core == 0
    for lane in range(2):
        angles = (base + (2 * chip + lane).astype(F32)) * freq_ref[...]
        cosine = jnp.where(is_key, jnp.cos(angles), 1.0)
        sine = jnp.where(is_key, jnp.sin(angles), 0.0)
        at = pl.ds(lane * ROWS, ROWS)
        cos[at, :] = cosine
        sin[at, :] = jnp.where(iota((ROWS, HD), 1) < HD // 2, -sine, sine)
    wz_take(1, 1)
    xa_wait(0)
    xb_start(range(3), 0)
    xa_start(1)

    q_in.wait()
    q_cols = H * HD // 2
    qp[...] = (
        jnp.dot(sel[:, :ROWS], qin[:, :q_cols], preferred_element_type=F32)
        + jnp.dot(sel[:, ROWS:], qin[:, q_cols:], preferred_element_type=F32)
    ).astype(BF16).reshape(qp.shape)

    def project(part):
        low, high = heads_of(part)
        wide = (high - low) * HD
        sums = sum(
            jnp.dot(
                hid[:, :, s * 1024 : (s + 1) * 1024].reshape(2 * ROWS, 1024),
                w[s, :, :, :, :, cols(part)].reshape(1024, wide),
                preferred_element_type=F32,
            )
            for s in range(4)
        )
        for b in range(low, high):
            at = pl.ds(b * HD, HD)
            rows = sums[:, (b - low) * HD : (b - low + 1) * HD]
            turned = (rows * cos[...] + pltpu.roll(rows, HD // 2, 1) * sin[...]).astype(BF16)
            kvp[:, :, at] = (
                jnp.dot(sel[...], turned, preferred_element_type=F32)
                .astype(BF16)
                .reshape(GROUPS, 16, HD)
            )

    def kv_copy(part, k):
        peer = lax.rem(g + k, GROUPS)
        return rdma(
            kvp.at[peer, :, cols(part)], rkv.at[chip, core, :, cols(part)],
            kv_sem.at[part, 0], kv_sem.at[part, 1], (peer, z),
        )

    def kv_take(part, way):
        take(kvp.at[0 : GROUPS - 1, :, cols(part)], kv_sem.at[part, way])

    def q_copy(k):
        peer = lax.rem(g + k, GROUPS)
        return rdma(qp.at[peer], rq.at[g], q_sem.at[0], q_sem.at[1], (peer, z))

    def q_take(way):
        take(qp.at[0 : GROUPS - 1], q_sem.at[way])

    def kv_begin(part):
        loop(1, GROUPS, lambda k: kv_copy(part, k).start())
        rkv[chip, core, :, cols(part)] = kvp[g, :, cols(part)]

    def kv_end(part):
        low, high = heads_of(part)
        slot = iota((SLOTS, 256), 0)
        col = iota((SLOTS, 256), 1)
        unpack = (slot == (col & 7) * GROUPS + (col >> 3)).astype(F32).astype(BF16)
        kv_take(part, 1)
        for kind in range(2):
            dense = jnp.dot(
                unpack,
                rkv[:, kind, :, cols(part)].reshape(256, (high - low) * HD),
                preferred_element_type=F32,
            )
            for b in range(low, high):
                buf[z, b, kind] = dense[:, (b - low) * HD : (b - low + 1) * HD].astype(BF16)

    above = lax.rem(z + 1, PIECES)
    below = lax.rem(z + PIECES - 1, PIECES)

    def ring_copy(way, step, b):
        if way == 0:
            piece, peer = lax.rem(z - step + PIECES, PIECES), above
        else:
            piece, peer = lax.rem(z + step, PIECES), below
        return rdma(
            buf.at[piece, b], buf.at[piece, b],
            ring_send.at[way, step, b], ring_recv.at[way, step, b], (g, peer),
        )

    def arrival(way, step, b):
        if way == 0:
            piece, peer = lax.rem(z - step - 1 + PIECES, PIECES), below
        else:
            piece, peer = lax.rem(z + step + 1, PIECES), above
        return rdma(
            buf.at[piece, b], buf.at[piece, b],
            ring_send.at[way, step, b], ring_recv.at[way, step, b], (g, peer),
        )

    def ring_begin(part):
        for b in range(*heads_of(part)):
            ring_copy(0, 0, b).start()
            ring_copy(1, 0, b).start()

    def relay(step, b):
        on = step < HALF - 2
        arrival(0, step, b).wait_recv()

        @pl.when(on | (lax.rem(b, 2) == 0))
        def _():
            ring_copy(0, step + 1, b).start()

        arrival(1, step, b).wait_recv()

        @pl.when(on | (lax.rem(b, 2) == 1))
        def _():
            ring_copy(1, step + 1, b).start()

    scale = HD ** -0.5 * LOG2E

    def block(pieces, b, mask):
        queries = qd[b]
        scores = [
            lax.dot_general(
                buf[piece, b, 0], queries, (((1,), (1,)), ((), ())), preferred_element_type=F32
            )
            * scale
            + bias[mask]
            for piece in pieces
        ]
        high = jnp.max(scores[0], axis=0, keepdims=True)
        for each in scores[1:]:
            high = jnp.maximum(high, jnp.max(each, axis=0, keepdims=True))
        if mask == 0:
            old = top[b, 0:1]
            high = jnp.maximum(old, high)
            fade = jnp.exp2(old - high)
        weights = [jnp.exp2(each - high) for each in scores]
        added = sum(jnp.sum(each, axis=0, keepdims=True) for each in weights)
        part = sum(
            lax.dot_general(
                buf[piece, b, 1], each.astype(BF16), (((0,), (0,)), ((), ())),
                preferred_element_type=F32,
            )
            for piece, each in zip(pieces, weights)
        )
        top[b, 0:1] = high
        if mask == 0:
            total[b, 0:1] = total[b, 0:1] * fade + added
            out_acc[b] = out_acc[b] * fade + part
        else:
            total[b, 0:1] = added
            out_acc[b] = part

    def attend(step, b):
        lower = z - step - 1
        upper = z + step + 1 - PIECES

        @pl.when(upper >= 0)
        def _():
            block((lower, upper), b, 0)

        @pl.when((upper < 0) & (lower >= 0))
        def _():
            block((lower,), b, 0)

    def attend_last(b):
        @pl.when(z >= HALF)
        def _():
            block((z - HALF,), b, 0)

    def emit(b):
        rows = jnp.transpose(out_acc[b] / total[b, 0:1])
        for h in range(SHARE):
            at = pl.ds(pl.multiple_of(b * (SHARE * HD), SHARE * HD) + h * HD, HD)
            o_ref[:, at] = jnp.where(
                live[...] > 0.5, rows[h * SLOTS : (h + 1) * SLOTS], 0.0
            ).astype(BF16)

    xa_wait(1)
    xb_wait(range(3), 0)
    xb_start(range(4), 1)
    hid_copy.wait_recv()
    project(0)
    kv_begin(0)
    for path in range(2):
        xb(1, path, 0).wait_recv()
        xb(1, path, 4).start()
        xb(1, path, 1).wait_recv()
        xb(1, path, 5).start()
    kv_end(0)
    ring_begin(0)
    relay(0, 0)

    unit_s = (iota((SLOTS, nseq), 0) >> 5).astype(F32)
    group = g.astype(F32)
    hit = (asg_r == group) & (offsets_r <= unit_s) & (unit_s < offsets_r + counts_r)
    seq_s = jnp.sum(
        jnp.where(hit, iota((SLOTS, nseq), 1) + 1, 0).astype(F32), axis=1, keepdims=True
    )

    def lane_slot(shape):
        lane = iota(shape, 1)
        for _ in range(SHARE - 1):
            lane = jnp.where(lane >= SLOTS, lane - SLOTS, lane)
        return lane

    unit_l = (lane_slot((nseq, WIDE)) >> 5).astype(F32)
    hit = (asg_c == group) & (offsets_c <= unit_l) & (unit_l < offsets_c + counts_c)
    seq_l = jnp.sum(
        jnp.where(hit, iota((nseq, WIDE), 0) + 1, 0).astype(F32), axis=0, keepdims=True
    )
    same = (seq_s == seq_l) & (seq_s > 0.5)
    bias[0] = jnp.where(same, 0.0, NEG_FILL)
    bias[1] = jnp.where(
        same & (iota((SLOTS, WIDE), 0) <= lane_slot((SLOTS, WIDE))), 0.0, NEG_FILL
    )
    live[...] = jnp.broadcast_to(seq_s, (SLOTS, HD))

    relay(1, 0)
    relay(2, 0)
    xb_wait(range(2, 6), 1)
    project(1)
    kv_begin(1)
    relay(3, 0)
    relay(4, 0)
    kv_end(1)
    ring_begin(1)
    loop(1, GROUPS, lambda k: q_copy(k).start())
    rq[g] = qp[g]
    relay(5, 0)
    relay(6, 0)
    loop(FIRST, KVH, lambda b: relay(0, b))
    arrival(0, HALF - 1, 0).wait_recv()
    loop(FIRST, KVH, lambda b: relay(1, b))
    q_take(1)
    arrived = rq[...].reshape(GROUPS * 16, q_cols)
    slot = iota((SLOTS, GROUPS * 16), 0)
    col = iota((SLOTS, GROUPS * 16), 1)
    for half in range(2):
        unpack = (slot == (col & 7) * GROUPS + (col >> 4)) & (((col >> 3) & 1) == half)
        dense = jnp.dot(unpack.astype(F32).astype(BF16), arrived, preferred_element_type=F32)
        for h in range(H // 2):
            head = half * (H // 2) + h
            qd[head // SHARE, pl.ds((head % SHARE) * SLOTS, SLOTS)] = dense[
                :, h * HD : (h + 1) * HD
            ].astype(BF16)

    loop(0, KVH, lambda b: block((z,), b, 1))

    rest = KVH - FIRST

    def steps(index):
        step = index // rest
        b = FIRST + lax.rem(index, rest)
        relay(step, b)
        attend(step - 2, b)

        @pl.when(b == FIRST)
        def _():
            attend(step, 0)

    loop(2 * rest, (HALF - 1) * rest, steps)
    loop(0, 2, lambda step: attend(step, 0))
    attend_last(0)
    emit(0)
    loop(FIRST, KVH, lambda b: attend(HALF - 3, b))
    loop(FIRST, KVH, lambda b: attend(HALF - 2, b))
    for b in range(FIRST, KVH):
        arrival(b % 2, HALF - 1, b).wait_recv()
        attend_last(b)
    loop(FIRST, KVH, emit)

    hid_copy.wait_send()
    for part in range(2):
        wz_take(part, 0)
        for path in range(2):
            for k in range(3):
                xa(part, path, k).wait_send()
            for kind in range(3 if part == 0 else 6):
                xb(part, path, kind).wait_send()
        kv_take(part, 0)
    q_take(0)

    def ring_sent(index):
        ring_copy(0, index // KVH, lax.rem(index, KVH)).wait_send()
        ring_copy(1, index // KVH, lax.rem(index, KVH)).wait_send()

    loop(0, (HALF - 1) * KVH, ring_sent)
    for b in range(KVH):
        ring_copy(b % 2, HALF - 1, b).wait_send()


def per_device(hidden, queries, key_weight, value_weight, lengths, assign):
    frequency = ROPE_BASE ** (-2.0 * np.arange(HD // 2) / HD)
    frequency = jnp.asarray(np.concatenate([frequency, frequency])[None], F32)
    vmem = pl.BlockSpec(memory_space=pltpu.VMEM)
    hbm = pl.BlockSpec(memory_space=pl.ANY)
    dma = pltpu.SemaphoreType.DMA
    out = pl.pallas_call(
        kernel,
        out_shape=jax.ShapeDtypeStruct((SLOTS, H * HD), BF16),
        in_specs=[hbm, hbm] + [vmem] * 5,
        out_specs=vmem,
        scratch_shapes=[
            pltpu.VMEM((2, ROWS, 4096), BF16),
            pltpu.VMEM((ROWS, H * HD), BF16),
            pltpu.VMEM((4, 4, 4, 4, 16, 512), BF16),
            pltpu.VMEM((GROUPS * 16, 2 * ROWS), BF16),
            pltpu.VMEM((2 * ROWS, HD), F32),
            pltpu.VMEM((2 * ROWS, HD), F32),
            pltpu.VMEM((GROUPS, 16, 512), BF16),
            pltpu.VMEM((GROUPS, 16, H * HD // 2), BF16),
            pltpu.VMEM((GROUPS // 2, 2, 16, 512), BF16),
            pltpu.VMEM((GROUPS, 16, H * HD // 2), BF16),
            pltpu.VMEM((KVH, WIDE, HD), BF16),
            pltpu.VMEM((PIECES, KVH, 2, SLOTS, HD), BF16),
            pltpu.VMEM((2, SLOTS, WIDE), F32),
            pltpu.VMEM((SLOTS, HD), F32),
            pltpu.VMEM((KVH, 8, WIDE), F32),
            pltpu.VMEM((KVH, 8, WIDE), F32),
            pltpu.VMEM((KVH, HD, WIDE), F32),
            dma((2,)),
            dma((2,)),
            dma((2, 2)),
            dma((2, 2, 2, 3)),
            dma((2, 2, 2, 6)),
            dma((2, 2)),
            dma((2,)),
            dma((2, HALF, KVH)),
            dma((2, HALF, KVH)),
        ],
        compiler_params=pltpu.CompilerParams(
            collective_id=0, has_side_effects=True, vmem_limit_bytes=VMEM_BYTES
        ),
        name="attend",
    )(
        hidden.reshape(ROWS, -1),
        queries.reshape(ROWS, -1),
        key_weight,
        value_weight,
        lengths.reshape(1, -1),
        assign.reshape(1, -1),
        frequency,
    )
    return out.reshape(1, SLOTS, H * HD)


def solution(mesh):
    return jax.shard_map(
        per_device,
        mesh=mesh,
        in_specs=(
            P(None, "grp", "sp"),
            P(None, "grp", "sp"),
            P("sp", None),
            P("sp", None),
            P(),
            P(),
        ),
        out_specs=P("grp", None, "sp"),
        check_vma=False,
    )
```

```python
import jax
import jax.numpy as jnp
import numpy as np
from jax import lax
from jax.experimental import pallas as pl
from jax.experimental.pallas import tpu as pltpu
from jax.sharding import PartitionSpec as P

H = 16
KVH = 4
SHARE = H // KVH
HD = 128
GROUPS = 32
PIECES = 16
ROWS = 128
SLOTS = 192
HALF = PIECES // 2
WIDE = SHARE * SLOTS
FIRST = 2
ROPE_BASE = 500000.0
NEG_FILL = -1e30
LOG2E = 1.4426950408889634
MESH = pl.DeviceIdType.MESH
VMEM_BYTES = 56 * 1024 * 1024
F32 = jnp.float32
BF16 = jnp.bfloat16


def iota(shape, dim):
    return lax.broadcasted_iota(jnp.int32, shape, dim)


def kernel(
    hid_ref, q_ref, wk_ref, wv_ref, len_ref, asg_ref, freq_ref,
    o_ref,
    hid, qin, w, sel, cos, sin, kvp, qp, rkv, rq, qd, buf, bias, live, top, total, out_acc,
    in_sem, hid_sem, wz_sem, xa_send, xa_sem, xb_send, xb_sem,
    kv_sem, q_sem, ring_send, ring_recv,
):
    g = lax.axis_index("grp")
    z = lax.axis_index("sp")
    core = lax.rem(g, 2)
    chip = g // 2
    x = lax.rem(chip, 4)
    y = chip // 4
    zq = z // 4
    zm = lax.rem(z, 4)

    def loop(low, high, act):
        def body(k, carry):
            act(k)
            return carry

        lax.fori_loop(low, high, body, 0)

    barrier = pltpu.get_barrier_semaphore()

    def greet(device):
        pl.semaphore_signal(barrier, inc=1, device_id=device, device_id_type=MESH)

    loop(1, PIECES, lambda k: greet((g, lax.rem(z + k, PIECES))))
    loop(1, GROUPS, lambda k: greet((lax.rem(g + k, GROUPS), z)))

    hid_in = pltpu.make_async_copy(hid_ref, hid.at[core], in_sem.at[0])
    q_in = pltpu.make_async_copy(q_ref, qin, in_sem.at[1])
    hid_in.start()
    q_in.start()
    own_rows = pl.ds(pl.multiple_of(chip * 16, 16), 16)
    w[zq, zm, y, x] = jnp.where(core == 0, wk_ref[own_rows, :], wv_ref[own_rows, :])

    nseq = len_ref.shape[1]
    first = iota((nseq, nseq), 0)
    second = iota((nseq, nseq), 1)
    diagonal = first == second
    counts_r = (len_ref[...] // (GROUPS * PIECES)).astype(F32)
    asg_r = asg_ref[...].astype(F32)
    counts_c = jnp.sum(jnp.where(diagonal, counts_r, 0.0), axis=1, keepdims=True)
    asg_c = jnp.sum(jnp.where(diagonal, asg_r, 0.0), axis=1, keepdims=True)
    same_group = asg_c == asg_r
    up_c = jnp.where(first < second, counts_c, 0.0)
    up_r = jnp.where(second < first, counts_r, 0.0)
    starts_r = jnp.sum(up_c, axis=0, keepdims=True)
    starts_c = jnp.sum(up_r, axis=1, keepdims=True)
    offsets_r = jnp.sum(jnp.where(same_group, up_c, 0.0), axis=0, keepdims=True)
    offsets_c = jnp.sum(jnp.where(same_group, up_r, 0.0), axis=1, keepdims=True)

    pl.semaphore_wait(barrier, GROUPS - 1 + PIECES - 1)

    def heads_of(part):
        return (0, FIRST) if part == 0 else (FIRST, KVH)

    def cols(part):
        low, high = heads_of(part)
        return pl.ds(low * HD, (high - low) * HD)

    def rdma(src, dst, send, recv, device):
        return pltpu.make_async_remote_copy(
            src_ref=src, dst_ref=dst, send_sem=send, recv_sem=recv,
            device_id=device, device_id_type=MESH,
        )

    def wz(part, step):
        slab = w.at[zq, zm, y, x, :, cols(part)]
        return rdma(
            slab, slab, wz_sem.at[part, 0], wz_sem.at[part, 1],
            (g, lax.rem(z + step, PIECES)),
        )

    def take(ref, sem):
        pltpu.make_async_copy(ref, ref, sem).wait()

    def wz_take(part, way):
        take(kvp.at[0 : PIECES - 1, :, cols(part)], wz_sem.at[part, way])

    def x_peer(step):
        return (2 * (y * 4 + lax.rem(x + step, 4)) + core, z)

    def y_peer(step):
        return (2 * (lax.rem(y + step, 4) * 4 + x) + core, z)

    def xa(part, path, k):
        slab = w.at[2 * path : 2 * path + 2, :, y, x, :, cols(part)]
        return rdma(
            slab, slab, xa_send.at[part], xa_sem.at[part, path, k],
            (x_peer, y_peer)[path]((2, 1, 3)[k]),
        )

    def xb_view(part, path, shards, place):
        if path == 0:
            return w.at[shards, :, place, :, :, cols(part)]
        return w.at[shards, :, :, place, :, cols(part)]

    def xb(part, path, kind):
        place = (y, x)[path]
        peer = (y_peer, x_peer)[path]
        low = 2 * path
        both, one, two = slice(low, low + 2), slice(low, low + 1), slice(low + 1, low + 2)
        if part == 0:
            slab, device = xb_view(part, path, both, place), peer((2, 1, 3)[kind])
        else:
            slab, device = (
                (xb_view(part, path, one, place), peer(1)),
                (xb_view(part, path, two, place), peer(3)),
                (xb_view(part, path, two, place), peer(1)),
                (xb_view(part, path, one, place), peer(3)),
                (xb_view(part, path, one, lax.rem(place + 3, 4)), peer(1)),
                (xb_view(part, path, two, lax.rem(place + 1, 4)), peer(3)),
            )[kind]
        return rdma(
            slab, slab, xb_send.at[part], xb_sem.at[part, path, kind], device
        )

    def xb_start(kinds, part):
        for path in range(2):
            for kind in kinds:
                xb(part, path, kind).start()

    def xb_wait(kinds, part):
        for path in range(2):
            for kind in kinds:
                xb(part, path, kind).wait_recv()

    def xa_start(part):
        for path in range(2):
            for k in range(3):
                xa(part, path, k).start()

    def xa_wait(part):
        for path in range(2):
            for k in range(3):
                xa(part, path, k).wait_recv()

    for part in range(2):
        for step in (8, 7, 9, 6, 10, 5, 11, 4, 12, 3, 13, 2, 14, 1, 15):
            wz(part, step).start()
    hid_in.wait()
    hid_copy = rdma(
        hid.at[core], hid.at[core], hid_sem.at[0], hid_sem.at[1], (g + 1 - 2 * core, z)
    )
    hid_copy.start()

    row_l = iota((nseq, ROWS), 1).astype(F32)
    here = (starts_c <= row_l) & (row_l < starts_c + counts_c)
    goal = jnp.sum(
        jnp.where(here, asg_c * 16.0 + offsets_c + row_l - starts_c, 0.0), axis=0, keepdims=True
    ).astype(jnp.int32)
    goal = jnp.concatenate([goal, goal + 8], axis=1)
    sel[...] = (iota((GROUPS * 16, 2 * ROWS), 0) == goal).astype(F32).astype(BF16)

    wz_take(0, 1)
    xa_start(0)
    row_s = iota((ROWS, nseq), 0).astype(F32)
    here = (starts_r <= row_s) & (row_s < starts_r + counts_r)
    base = jnp.sum(
        jnp.where(
            here,
            z.astype(F32) * counts_r * GROUPS + (row_s - starts_r) * GROUPS,
            0.0,
        ),
        axis=1, keepdims=True,
    )
    is_key = core == 0
    for lane in range(2):
        angles = (base + (2 * chip + lane).astype(F32)) * freq_ref[...]
        cosine = jnp.where(is_key, jnp.cos(angles), 1.0)
        sine = jnp.where(is_key, jnp.sin(angles), 0.0)
        at = pl.ds(lane * ROWS, ROWS)
        cos[at, :] = cosine
        sin[at, :] = jnp.where(iota((ROWS, HD), 1) < HD // 2, -sine, sine)
    wz_take(1, 1)
    xa_wait(0)
    xb_start(range(3), 0)
    xa_start(1)

    q_in.wait()
    q_cols = H * HD // 2
    qp[...] = (
        jnp.dot(sel[:, :ROWS], qin[:, :q_cols], preferred_element_type=F32)
        + jnp.dot(sel[:, ROWS:], qin[:, q_cols:], preferred_element_type=F32)
    ).astype(BF16).reshape(qp.shape)

    def project(part):
        low, high = heads_of(part)
        wide = (high - low) * HD
        sums = sum(
            jnp.dot(
                hid[:, :, s * 1024 : (s + 1) * 1024].reshape(2 * ROWS, 1024),
                w[s, :, :, :, :, cols(part)].reshape(1024, wide),
                preferred_element_type=F32,
            )
            for s in range(4)
        )
        for b in range(low, high):
            at = pl.ds(b * HD, HD)
            rows = sums[:, (b - low) * HD : (b - low + 1) * HD]
            turned = (rows * cos[...] + pltpu.roll(rows, HD // 2, 1) * sin[...]).astype(BF16)
            kvp[:, :, at] = (
                jnp.dot(sel[...], turned, preferred_element_type=F32)
                .astype(BF16)
                .reshape(GROUPS, 16, HD)
            )

    def kv_copy(part, k):
        peer = lax.rem(g + k, GROUPS)
        return rdma(
            kvp.at[peer, :, cols(part)], rkv.at[chip, core, :, cols(part)],
            kv_sem.at[part, 0], kv_sem.at[part, 1], (peer, z),
        )

    def kv_take(part, way):
        take(kvp.at[0 : GROUPS - 1, :, cols(part)], kv_sem.at[part, way])

    def q_copy(k):
        peer = lax.rem(g + k, GROUPS)
        return rdma(qp.at[peer], rq.at[g], q_sem.at[0], q_sem.at[1], (peer, z))

    def q_take(way):
        take(qp.at[0 : GROUPS - 1], q_sem.at[way])

    def kv_begin(part):
        loop(1, GROUPS, lambda k: kv_copy(part, k).start())
        rkv[chip, core, :, cols(part)] = kvp[g, :, cols(part)]

    def kv_end(part):
        low, high = heads_of(part)
        slot = iota((SLOTS, 256), 0)
        col = iota((SLOTS, 256), 1)
        unpack = (slot == (col & 7) * GROUPS + (col >> 3)).astype(F32).astype(BF16)
        kv_take(part, 1)
        for kind in range(2):
            dense = jnp.dot(
                unpack,
                rkv[:, kind, :, cols(part)].reshape(256, (high - low) * HD),
                preferred_element_type=F32,
            )
            for b in range(low, high):
                buf[z, b, kind] = dense[:, (b - low) * HD : (b - low + 1) * HD].astype(BF16)

    above = lax.rem(z + 1, PIECES)
    below = lax.rem(z + PIECES - 1, PIECES)

    def ring_copy(way, step, b, kind):
        if way == 0:
            piece, peer = lax.rem(z - step + PIECES, PIECES), above
        else:
            piece, peer = lax.rem(z + step, PIECES), below
        return rdma(
            buf.at[piece, b, kind], buf.at[piece, b, kind],
            ring_send.at[way], ring_recv.at[way, step, b, kind], (g, peer),
        )

    def arrival(way, step, b, kind):
        if way == 0:
            piece, peer = lax.rem(z - step - 1 + PIECES, PIECES), below
        else:
            piece, peer = lax.rem(z + step + 1, PIECES), above
        return rdma(
            buf.at[piece, b, kind], buf.at[piece, b, kind],
            ring_send.at[way], ring_recv.at[way, step, b, kind], (g, peer),
        )

    def ring_begin(part):
        for b in range(*heads_of(part)):
            for kind in range(2):
                ring_copy(0, 0, b, kind).start()
                ring_copy(1, 0, b, kind).start()

    def relay(step, b):
        on = step < HALF - 2
        for kind in range(2):
            for way in range(2):
                arrival(way, step, b, kind).wait_recv()
                if way == kind:
                    ring_copy(way, step + 1, b, kind).start()
                else:

                    @pl.when(on)
                    def _():
                        ring_copy(way, step + 1, b, kind).start()

    def last_wait(b):
        for kind in range(2):
            arrival(kind, HALF - 1, b, kind).wait_recv()

    scale = HD ** -0.5 * LOG2E

    def block(pieces, b, mask):
        queries = qd[b]
        scores = [
            lax.dot_general(
                buf[piece, b, 0], queries, (((1,), (1,)), ((), ())), preferred_element_type=F32
            )
            * scale
            + bias[mask]
            for piece in pieces
        ]
        high = jnp.max(scores[0], axis=0, keepdims=True)
        for each in scores[1:]:
            high = jnp.maximum(high, jnp.max(each, axis=0, keepdims=True))
        if mask == 0:
            old = top[b, 0:1]
            high = jnp.maximum(old, high)
            fade = jnp.exp2(old - high)
        weights = [jnp.exp2(each - high) for each in scores]
        added = sum(jnp.sum(each, axis=0, keepdims=True) for each in weights)
        part = sum(
            lax.dot_general(
                buf[piece, b, 1], each.astype(BF16), (((0,), (0,)), ((), ())),
                preferred_element_type=F32,
            )
            for piece, each in zip(pieces, weights)
        )
        top[b, 0:1] = high
        if mask == 0:
            total[b, 0:1] = total[b, 0:1] * fade + added
            out_acc[b] = out_acc[b] * fade + part
        else:
            total[b, 0:1] = added
            out_acc[b] = part

    def attend(step, b):
        lower = z - step - 1
        upper = z + step + 1 - PIECES

        @pl.when(upper >= 0)
        def _():
            block((lower, upper), b, 0)

        @pl.when((upper < 0) & (lower >= 0))
        def _():
            block((lower,), b, 0)

    def attend_last(b):
        @pl.when(z >= HALF)
        def _():
            block((z - HALF,), b, 0)

    def emit(b):
        rows = jnp.transpose(out_acc[b] * (1.0 / total[b, 0:1]))
        for h in range(SHARE):
            at = pl.ds(pl.multiple_of(b * (SHARE * HD), SHARE * HD) + h * HD, HD)
            o_ref[:, at] = jnp.where(
                live[...] > 0.5, rows[h * SLOTS : (h + 1) * SLOTS], 0.0
            ).astype(BF16)

    xa_wait(1)
    xb_wait(range(3), 0)
    xb_start(range(4), 1)
    hid_copy.wait_recv()
    project(0)
    kv_begin(0)
    for path in range(2):
        xb(1, path, 0).wait_recv()
        xb(1, path, 4).start()
        xb(1, path, 1).wait_recv()
        xb(1, path, 5).start()
    kv_end(0)
    ring_begin(0)
    loop(0, FIRST, lambda b: relay(0, b))

    unit_s = (iota((SLOTS, nseq), 0) >> 5).astype(F32)
    group = g.astype(F32)
    hit = (asg_r == group) & (offsets_r <= unit_s) & (unit_s < offsets_r + counts_r)
    seq_s = jnp.sum(
        jnp.where(hit, iota((SLOTS, nseq), 1) + 1, 0).astype(F32), axis=1, keepdims=True
    )

    def lane_slot(shape):
        lane = iota(shape, 1)
        for _ in range(SHARE - 1):
            lane = jnp.where(lane >= SLOTS, lane - SLOTS, lane)
        return lane

    unit_l = (lane_slot((nseq, WIDE)) >> 5).astype(F32)
    hit = (asg_c == group) & (offsets_c <= unit_l) & (unit_l < offsets_c + counts_c)
    seq_l = jnp.sum(
        jnp.where(hit, iota((nseq, WIDE), 0) + 1, 0).astype(F32), axis=0, keepdims=True
    )
    same = (seq_s == seq_l) & (seq_s > 0.5)
    bias[0] = jnp.where(same, 0.0, NEG_FILL)
    bias[1] = jnp.where(
        same & (iota((SLOTS, WIDE), 0) <= lane_slot((SLOTS, WIDE))), 0.0, NEG_FILL
    )
    live[...] = jnp.broadcast_to(seq_s, (SLOTS, HD))

    loop(0, FIRST, lambda b: relay(1, b))
    xb_wait(range(2, 6), 1)
    project(1)
    kv_begin(1)
    loop(0, FIRST, lambda b: relay(2, b))
    kv_end(1)
    ring_begin(1)
    loop(0, FIRST, lambda b: relay(3, b))
    loop(1, GROUPS, lambda k: q_copy(k).start())
    rq[g] = qp[g]
    loop(0, FIRST, lambda b: relay(4, b))
    loop(FIRST, KVH, lambda b: relay(0, b))
    loop(0, FIRST, lambda b: relay(5, b))
    loop(FIRST, KVH, lambda b: relay(1, b))
    loop(0, FIRST, lambda b: relay(6, b))
    q_take(1)
    arrived = rq[...].reshape(GROUPS * 16, q_cols)
    slot = iota((SLOTS, GROUPS * 16), 0)
    col = iota((SLOTS, GROUPS * 16), 1)
    for half in range(2):
        unpack = (slot == (col & 7) * GROUPS + (col >> 4)) & (((col >> 3) & 1) == half)
        dense = jnp.dot(unpack.astype(F32).astype(BF16), arrived, preferred_element_type=F32)
        for h in range(H // 2):
            head = half * (H // 2) + h
            qd[head // SHARE, pl.ds((head % SHARE) * SLOTS, SLOTS)] = dense[
                :, h * HD : (h + 1) * HD
            ].astype(BF16)

    loop(0, KVH, lambda b: block((z,), b, 1))

    rest = KVH - FIRST

    def steps(index):
        step = index // rest
        b = FIRST + lax.rem(index, rest)
        relay(step, b)
        attend(step - 2, b)

        @pl.when(b == FIRST)
        def _():
            loop(0, FIRST, lambda c: attend(step, c))

    loop(2 * rest, (HALF - 1) * rest, steps)
    loop(0, FIRST, lambda b: attend(0, b))
    loop(0, FIRST, lambda b: attend(1, b))
    for b in range(FIRST):
        last_wait(b)
        attend_last(b)
    loop(0, FIRST, emit)
    loop(FIRST, KVH, lambda b: attend(HALF - 3, b))
    loop(FIRST, KVH, lambda b: attend(HALF - 2, b))
    for b in range(FIRST, KVH):
        last_wait(b)
        attend_last(b)
    loop(FIRST, KVH, emit)

    hid_copy.wait_send()
    q_take(0)
    for part in range(2):
        wz_take(part, 0)
        kv_take(part, 0)
        take(w.at[0:3, :, :, 0, :, cols(part)], xa_send.at[part])
        take(w.at[0:3, :, :, :, :, cols(part)], xb_send.at[part])
    for way in range(2):
        take(buf.at[0 : HALF - 1], ring_send.at[way])
        take(buf.at[0, :, 0], ring_send.at[way])


def per_device(hidden, queries, key_weight, value_weight, lengths, assign):
    frequency = ROPE_BASE ** (-2.0 * np.arange(HD // 2) / HD)
    frequency = jnp.asarray(np.concatenate([frequency, frequency])[None], F32)
    vmem = pl.BlockSpec(memory_space=pltpu.VMEM)
    hbm = pl.BlockSpec(memory_space=pl.ANY)
    dma = pltpu.SemaphoreType.DMA
    out = pl.pallas_call(
        kernel,
        out_shape=jax.ShapeDtypeStruct((SLOTS, H * HD), BF16),
        in_specs=[hbm, hbm] + [vmem] * 5,
        out_specs=vmem,
        scratch_shapes=[
            pltpu.VMEM((2, ROWS, 4096), BF16),
            pltpu.VMEM((ROWS, H * HD), BF16),
            pltpu.VMEM((4, 4, 4, 4, 16, 512), BF16),
            pltpu.VMEM((GROUPS * 16, 2 * ROWS), BF16),
            pltpu.VMEM((2 * ROWS, HD), F32),
            pltpu.VMEM((2 * ROWS, HD), F32),
            pltpu.VMEM((GROUPS, 16, 512), BF16),
            pltpu.VMEM((GROUPS, 16, H * HD // 2), BF16),
            pltpu.VMEM((GROUPS // 2, 2, 16, 512), BF16),
            pltpu.VMEM((GROUPS, 16, H * HD // 2), BF16),
            pltpu.VMEM((KVH, WIDE, HD), BF16),
            pltpu.VMEM((PIECES, KVH, 2, SLOTS, HD), BF16),
            pltpu.VMEM((2, SLOTS, WIDE), F32),
            pltpu.VMEM((SLOTS, HD), F32),
            pltpu.VMEM((KVH, 8, WIDE), F32),
            pltpu.VMEM((KVH, 8, WIDE), F32),
            pltpu.VMEM((KVH, HD, WIDE), F32),
            dma((2,)),
            dma((2,)),
            dma((2, 2)),
            dma((2,)),
            dma((2, 2, 3)),
            dma((2,)),
            dma((2, 2, 6)),
            dma((2, 2)),
            dma((2,)),
            dma((2,)),
            dma((2, HALF, KVH, 2)),
        ],
        compiler_params=pltpu.CompilerParams(
            collective_id=0, has_side_effects=True, vmem_limit_bytes=VMEM_BYTES
        ),
        name="attend",
    )(
        hidden.reshape(ROWS, -1),
        queries.reshape(ROWS, -1),
        key_weight,
        value_weight,
        lengths.reshape(1, -1),
        assign.reshape(1, -1),
        frequency,
    )
    return out.reshape(1, SLOTS, H * HD)


def solution(mesh):
    return jax.shard_map(
        per_device,
        mesh=mesh,
        in_specs=(
            P(None, "grp", "sp"),
            P(None, "grp", "sp"),
            P("sp", None),
            P("sp", None),
            P(),
            P(),
        ),
        out_specs=P("grp", None, "sp"),
        check_vma=False,
    )
```

```python
import jax
import jax.numpy as jnp
import numpy as np
from jax import lax
from jax.experimental import pallas as pl
from jax.experimental.pallas import tpu as pltpu
from jax.sharding import PartitionSpec as P

H = 16
KVH = 4
SHARE = H // KVH
HD = 128
GROUPS = 32
PIECES = 16
ROWS = 128
SLOTS = 192
HALF = PIECES // 2
WIDE = SHARE * SLOTS
FIRST = 2
ROPE_BASE = 500000.0
NEG_FILL = -1e30
LOG2E = 1.4426950408889634
MESH = pl.DeviceIdType.MESH
VMEM_BYTES = 56 * 1024 * 1024
F32 = jnp.float32
BF16 = jnp.bfloat16


def iota(shape, dim):
    return lax.broadcasted_iota(jnp.int32, shape, dim)


def kernel(
    hid_ref, q_ref, wk_ref, wv_ref, len_ref, asg_ref, freq_ref,
    o_ref,
    hid, qin, w, sel, cos, sin, kvp, qp, rkv, rq, qd, buf, bias, live, top, total, out_acc,
    in_sem, hid_sem, wz_sem, xa_send, xa_sem, xb_send, xb_sem,
    kv_sem, q_sem, ring_send, ring_recv,
):
    g = lax.axis_index("grp")
    z = lax.axis_index("sp")
    core = lax.rem(g, 2)
    chip = g // 2
    x = lax.rem(chip, 4)
    y = chip // 4
    zq = z // 4
    zm = lax.rem(z, 4)

    def loop(low, high, act):
        def body(k, carry):
            act(k)
            return carry

        lax.fori_loop(low, high, body, 0)

    barrier = pltpu.get_barrier_semaphore()

    def greet(device):
        pl.semaphore_signal(barrier, inc=1, device_id=device, device_id_type=MESH)

    loop(1, PIECES, lambda k: greet((g, lax.rem(z + k, PIECES))))
    loop(1, GROUPS, lambda k: greet((lax.rem(g + k, GROUPS), z)))

    hid_in = pltpu.make_async_copy(hid_ref, hid.at[core], in_sem.at[0])
    q_in = pltpu.make_async_copy(q_ref, qin, in_sem.at[1])
    hid_in.start()
    q_in.start()
    own_rows = pl.ds(pl.multiple_of(chip * 16, 16), 16)
    w[zq, zm, y, x] = jnp.where(core == 0, wk_ref[own_rows, :], wv_ref[own_rows, :])

    nseq = len_ref.shape[1]
    first = iota((nseq, nseq), 0)
    second = iota((nseq, nseq), 1)
    diagonal = first == second
    counts_r = (len_ref[...] // (GROUPS * PIECES)).astype(F32)
    asg_r = asg_ref[...].astype(F32)
    counts_c = jnp.sum(jnp.where(diagonal, counts_r, 0.0), axis=1, keepdims=True)
    asg_c = jnp.sum(jnp.where(diagonal, asg_r, 0.0), axis=1, keepdims=True)
    same_group = asg_c == asg_r
    up_c = jnp.where(first < second, counts_c, 0.0)
    up_r = jnp.where(second < first, counts_r, 0.0)
    starts_r = jnp.sum(up_c, axis=0, keepdims=True)
    starts_c = jnp.sum(up_r, axis=1, keepdims=True)
    offsets_r = jnp.sum(jnp.where(same_group, up_c, 0.0), axis=0, keepdims=True)
    offsets_c = jnp.sum(jnp.where(same_group, up_r, 0.0), axis=1, keepdims=True)

    pl.semaphore_wait(barrier, GROUPS - 1 + PIECES - 1)

    def heads_of(part):
        return (0, FIRST) if part == 0 else (FIRST, KVH)

    def cols(part):
        low, high = heads_of(part)
        return pl.ds(low * HD, (high - low) * HD)

    def rdma(src, dst, send, recv, device):
        return pltpu.make_async_remote_copy(
            src_ref=src, dst_ref=dst, send_sem=send, recv_sem=recv,
            device_id=device, device_id_type=MESH,
        )

    def wz(part, step):
        slab = w.at[zq, zm, y, x, :, cols(part)]
        return rdma(
            slab, slab, wz_sem.at[part, 0], wz_sem.at[part, 1],
            (g, lax.rem(z + step, PIECES)),
        )

    def take(ref, sem):
        pltpu.make_async_copy(ref, ref, sem).wait()

    def wz_take(part, way):
        take(kvp.at[0 : PIECES - 1, :, cols(part)], wz_sem.at[part, way])

    def x_peer(step):
        return (2 * (y * 4 + lax.rem(x + step, 4)) + core, z)

    def y_peer(step):
        return (2 * (lax.rem(y + step, 4) * 4 + x) + core, z)

    def xa(part, path, k):
        slab = w.at[2 * path : 2 * path + 2, :, y, x, :, cols(part)]
        return rdma(
            slab, slab, xa_send.at[part], xa_sem.at[part, path, k],
            (x_peer, y_peer)[path]((2, 1, 3)[k]),
        )

    def xb_view(part, path, shards, place):
        if path == 0:
            return w.at[shards, :, place, :, :, cols(part)]
        return w.at[shards, :, :, place, :, cols(part)]

    def xb(part, path, kind):
        place = (y, x)[path]
        peer = (y_peer, x_peer)[path]
        low = 2 * path
        one, two = slice(low, low + 1), slice(low + 1, low + 2)
        slab, device = (
            (xb_view(part, path, one, place), peer(1)),
            (xb_view(part, path, two, place), peer(3)),
            (xb_view(part, path, two, place), peer(1)),
            (xb_view(part, path, one, place), peer(3)),
            (xb_view(part, path, one, lax.rem(place + 3, 4)), peer(1)),
            (xb_view(part, path, two, lax.rem(place + 1, 4)), peer(3)),
        )[kind]
        return rdma(
            slab, slab, xb_send.at[part], xb_sem.at[part, path, kind], device
        )

    def xb_start(kinds, part):
        for path in range(2):
            for kind in kinds:
                xb(part, path, kind).start()

    def xb_wait(kinds, part):
        for path in range(2):
            for kind in kinds:
                xb(part, path, kind).wait_recv()

    def xb_relay(part):
        for path in range(2):
            xb(part, path, 0).wait_recv()
            xb(part, path, 4).start()
            xb(part, path, 1).wait_recv()
            xb(part, path, 5).start()

    def xa_start(part):
        for path in range(2):
            for k in range(3):
                xa(part, path, k).start()

    def xa_wait(part):
        for path in range(2):
            for k in range(3):
                xa(part, path, k).wait_recv()

    for part in range(2):
        for step in (8, 7, 9, 6, 10, 5, 11, 4, 12, 3, 13, 2, 14, 1, 15):
            wz(part, step).start()
    hid_in.wait()
    hid_copy = rdma(
        hid.at[core], hid.at[core], hid_sem.at[0], hid_sem.at[1], (g + 1 - 2 * core, z)
    )
    hid_copy.start()

    row_l = iota((nseq, ROWS), 1).astype(F32)
    here = (starts_c <= row_l) & (row_l < starts_c + counts_c)
    goal = jnp.sum(
        jnp.where(here, asg_c * 16.0 + offsets_c + row_l - starts_c, 0.0), axis=0, keepdims=True
    ).astype(jnp.int32)
    goal = jnp.concatenate([goal, goal + 8], axis=1)
    sel[...] = (iota((GROUPS * 16, 2 * ROWS), 0) == goal).astype(F32).astype(BF16)

    wz_take(0, 1)
    xa_start(0)
    row_s = iota((ROWS, nseq), 0).astype(F32)
    here = (starts_r <= row_s) & (row_s < starts_r + counts_r)
    base = jnp.sum(
        jnp.where(
            here,
            z.astype(F32) * counts_r * GROUPS + (row_s - starts_r) * GROUPS,
            0.0,
        ),
        axis=1, keepdims=True,
    )
    is_key = core == 0
    for lane in range(2):
        angles = (base + (2 * chip + lane).astype(F32)) * freq_ref[...]
        cosine = jnp.where(is_key, jnp.cos(angles), 1.0)
        sine = jnp.where(is_key, jnp.sin(angles), 0.0)
        at = pl.ds(lane * ROWS, ROWS)
        cos[at, :] = cosine
        sin[at, :] = jnp.where(iota((ROWS, HD), 1) < HD // 2, -sine, sine)
    wz_take(1, 1)
    xa_start(1)
    xa_wait(0)
    xb_start(range(4), 0)

    q_in.wait()
    q_cols = H * HD // 2
    qp[...] = (
        jnp.dot(sel[:, :ROWS], qin[:, :q_cols], preferred_element_type=F32)
        + jnp.dot(sel[:, ROWS:], qin[:, q_cols:], preferred_element_type=F32)
    ).astype(BF16).reshape(qp.shape)

    def project(part):
        low, high = heads_of(part)
        wide = (high - low) * HD
        sums = sum(
            jnp.dot(
                hid[:, :, s * 1024 : (s + 1) * 1024].reshape(2 * ROWS, 1024),
                w[s, :, :, :, :, cols(part)].reshape(1024, wide),
                preferred_element_type=F32,
            )
            for s in range(4)
        )
        for b in range(low, high):
            at = pl.ds(b * HD, HD)
            rows = sums[:, (b - low) * HD : (b - low + 1) * HD]
            turned = (rows * cos[...] + pltpu.roll(rows, HD // 2, 1) * sin[...]).astype(BF16)
            kvp[:, :, at] = (
                jnp.dot(sel[...], turned, preferred_element_type=F32)
                .astype(BF16)
                .reshape(GROUPS, 16, HD)
            )

    def kv_copy(part, k):
        peer = lax.rem(g + k, GROUPS)
        return rdma(
            kvp.at[peer, :, cols(part)], rkv.at[chip, core, :, cols(part)],
            kv_sem.at[part, 0], kv_sem.at[part, 1], (peer, z),
        )

    def kv_take(part, way):
        take(kvp.at[0 : GROUPS - 1, :, cols(part)], kv_sem.at[part, way])

    def q_copy(k):
        peer = lax.rem(g + k, GROUPS)
        return rdma(qp.at[peer], rq.at[g], q_sem.at[0], q_sem.at[1], (peer, z))

    def q_take(way):
        take(qp.at[0 : GROUPS - 1], q_sem.at[way])

    def kv_begin(part):
        loop(1, GROUPS, lambda k: kv_copy(part, k).start())
        rkv[chip, core, :, cols(part)] = kvp[g, :, cols(part)]

    def kv_end(part):
        low, high = heads_of(part)
        slot = iota((SLOTS, 256), 0)
        col = iota((SLOTS, 256), 1)
        unpack = (slot == (col & 7) * GROUPS + (col >> 3)).astype(F32).astype(BF16)
        kv_take(part, 1)
        for kind in range(2):
            dense = jnp.dot(
                unpack,
                rkv[:, kind, :, cols(part)].reshape(256, (high - low) * HD),
                preferred_element_type=F32,
            )
            for b in range(low, high):
                buf[z, b, kind] = dense[:, (b - low) * HD : (b - low + 1) * HD].astype(BF16)

    above = lax.rem(z + 1, PIECES)
    below = lax.rem(z + PIECES - 1, PIECES)

    def ring_copy(way, step, b, kind):
        if way == 0:
            piece, peer = lax.rem(z - step + PIECES, PIECES), above
        else:
            piece, peer = lax.rem(z + step, PIECES), below
        return rdma(
            buf.at[piece, b, kind], buf.at[piece, b, kind],
            ring_send.at[way], ring_recv.at[way, step, b, kind], (g, peer),
        )

    def arrival(way, step, b, kind):
        if way == 0:
            piece, peer = lax.rem(z - step - 1 + PIECES, PIECES), below
        else:
            piece, peer = lax.rem(z + step + 1, PIECES), above
        return rdma(
            buf.at[piece, b, kind], buf.at[piece, b, kind],
            ring_send.at[way], ring_recv.at[way, step, b, kind], (g, peer),
        )

    def ring_begin(part):
        for b in range(*heads_of(part)):
            for kind in range(2):
                ring_copy(0, 0, b, kind).start()
                ring_copy(1, 0, b, kind).start()

    def relay(step, b):
        on = step < HALF - 2
        for kind in range(2):
            for way in range(2):
                arrival(way, step, b, kind).wait_recv()
                if way == kind:
                    ring_copy(way, step + 1, b, kind).start()
                else:

                    @pl.when(on)
                    def _():
                        ring_copy(way, step + 1, b, kind).start()

    def last_wait(b):
        for kind in range(2):
            arrival(kind, HALF - 1, b, kind).wait_recv()

    scale = HD ** -0.5 * LOG2E

    def block(pieces, b, mask):
        queries = qd[b]
        scores = [
            lax.dot_general(
                buf[piece, b, 0], queries, (((1,), (1,)), ((), ())), preferred_element_type=F32
            )
            * scale
            + bias[mask]
            for piece in pieces
        ]
        high = jnp.max(scores[0], axis=0, keepdims=True)
        for each in scores[1:]:
            high = jnp.maximum(high, jnp.max(each, axis=0, keepdims=True))
        if mask == 0:
            old = top[b, 0:1]
            high = jnp.maximum(old, high)
            fade = jnp.exp2(old - high)
        weights = [jnp.exp2(each - high) for each in scores]
        added = sum(jnp.sum(each, axis=0, keepdims=True) for each in weights)
        part = sum(
            lax.dot_general(
                buf[piece, b, 1], each.astype(BF16), (((0,), (0,)), ((), ())),
                preferred_element_type=F32,
            )
            for piece, each in zip(pieces, weights)
        )
        top[b, 0:1] = high
        if mask == 0:
            total[b, 0:1] = total[b, 0:1] * fade + added
            out_acc[b] = out_acc[b] * fade + part
        else:
            total[b, 0:1] = added
            out_acc[b] = part

    def attend(step, b):
        lower = z - step - 1
        upper = z + step + 1 - PIECES

        @pl.when(upper >= 0)
        def _():
            block((lower, upper), b, 0)

        @pl.when((upper < 0) & (lower >= 0))
        def _():
            block((lower,), b, 0)

    def attend_last(b):
        @pl.when(z >= HALF)
        def _():
            block((z - HALF,), b, 0)

    def emit(b):
        rows = jnp.transpose(out_acc[b] * (1.0 / total[b, 0:1]))
        for h in range(SHARE):
            at = pl.ds(pl.multiple_of(b * (SHARE * HD), SHARE * HD) + h * HD, HD)
            o_ref[:, at] = jnp.where(
                live[...] > 0.5, rows[h * SLOTS : (h + 1) * SLOTS], 0.0
            ).astype(BF16)

    xb_relay(0)
    xa_wait(1)
    xb_start(range(4), 1)
    xb_wait(range(2, 6), 0)
    hid_copy.wait_recv()
    project(0)
    kv_begin(0)
    xb_relay(1)
    kv_end(0)
    ring_begin(0)
    loop(0, FIRST, lambda b: relay(0, b))

    unit_s = (iota((SLOTS, nseq), 0) >> 5).astype(F32)
    group = g.astype(F32)
    hit = (asg_r == group) & (offsets_r <= unit_s) & (unit_s < offsets_r + counts_r)
    seq_s = jnp.sum(
        jnp.where(hit, iota((SLOTS, nseq), 1) + 1, 0).astype(F32), axis=1, keepdims=True
    )

    def lane_slot(shape):
        lane = iota(shape, 1)
        for _ in range(SHARE - 1):
            lane = jnp.where(lane >= SLOTS, lane - SLOTS, lane)
        return lane

    unit_l = (lane_slot((nseq, WIDE)) >> 5).astype(F32)
    hit = (asg_c == group) & (offsets_c <= unit_l) & (unit_l < offsets_c + counts_c)
    seq_l = jnp.sum(
        jnp.where(hit, iota((nseq, WIDE), 0) + 1, 0).astype(F32), axis=0, keepdims=True
    )
    same = (seq_s == seq_l) & (seq_s > 0.5)
    bias[0] = jnp.where(same, 0.0, NEG_FILL)
    bias[1] = jnp.where(
        same & (iota((SLOTS, WIDE), 0) <= lane_slot((SLOTS, WIDE))), 0.0, NEG_FILL
    )
    live[...] = jnp.broadcast_to(seq_s, (SLOTS, HD))

    xb_wait(range(2, 6), 1)
    project(1)
    kv_begin(1)
    loop(0, FIRST, lambda b: relay(1, b))
    loop(0, FIRST, lambda b: relay(2, b))
    kv_end(1)
    ring_begin(1)
    loop(0, FIRST, lambda b: relay(3, b))
    loop(1, GROUPS, lambda k: q_copy(k).start())
    rq[g] = qp[g]
    loop(0, FIRST, lambda b: relay(4, b))
    loop(FIRST, KVH, lambda b: relay(0, b))
    loop(0, FIRST, lambda b: relay(5, b))
    loop(FIRST, KVH, lambda b: relay(1, b))
    loop(0, FIRST, lambda b: relay(6, b))
    q_take(1)
    arrived = rq[...].reshape(GROUPS * 16, q_cols)
    slot = iota((SLOTS, GROUPS * 16), 0)
    col = iota((SLOTS, GROUPS * 16), 1)
    for half in range(2):
        unpack = (slot == (col & 7) * GROUPS + (col >> 4)) & (((col >> 3) & 1) == half)
        dense = jnp.dot(unpack.astype(F32).astype(BF16), arrived, preferred_element_type=F32)
        for h in range(H // 2):
            head = half * (H // 2) + h
            qd[head // SHARE, pl.ds((head % SHARE) * SLOTS, SLOTS)] = dense[
                :, h * HD : (h + 1) * HD
            ].astype(BF16)

    loop(0, KVH, lambda b: block((z,), b, 1))

    rest = KVH - FIRST

    def steps(index):
        step = index // rest
        b = FIRST + lax.rem(index, rest)
        relay(step, b)
        attend(step - 2, b)

        @pl.when(b == FIRST)
        def _():
            loop(0, FIRST, lambda c: attend(step, c))

    loop(2 * rest, (HALF - 1) * rest, steps)
    loop(0, FIRST, lambda b: attend(0, b))
    loop(0, FIRST, lambda b: attend(1, b))
    for b in range(FIRST):
        last_wait(b)
        attend_last(b)
    loop(0, FIRST, emit)
    loop(FIRST, KVH, lambda b: attend(HALF - 3, b))
    loop(FIRST, KVH, lambda b: attend(HALF - 2, b))
    for b in range(FIRST, KVH):
        last_wait(b)
        attend_last(b)
    loop(FIRST, KVH, emit)

    hid_copy.wait_send()
    q_take(0)
    for part in range(2):
        wz_take(part, 0)
        kv_take(part, 0)
        take(w.at[0:3, :, :, 0, :, cols(part)], xa_send.at[part])
        take(w.at[0:3, :, :, :, :, cols(part)], xb_send.at[part])
    for way in range(2):
        take(buf.at[0 : HALF - 1], ring_send.at[way])
        take(buf.at[0, :, 0], ring_send.at[way])


def per_device(hidden, queries, key_weight, value_weight, lengths, assign):
    frequency = ROPE_BASE ** (-2.0 * np.arange(HD // 2) / HD)
    frequency = jnp.asarray(np.concatenate([frequency, frequency])[None], F32)
    vmem = pl.BlockSpec(memory_space=pltpu.VMEM)
    hbm = pl.BlockSpec(memory_space=pl.ANY)
    dma = pltpu.SemaphoreType.DMA
    out = pl.pallas_call(
        kernel,
        out_shape=jax.ShapeDtypeStruct((SLOTS, H * HD), BF16),
        in_specs=[hbm, hbm] + [vmem] * 5,
        out_specs=vmem,
        scratch_shapes=[
            pltpu.VMEM((2, ROWS, 4096), BF16),
            pltpu.VMEM((ROWS, H * HD), BF16),
            pltpu.VMEM((4, 4, 4, 4, 16, 512), BF16),
            pltpu.VMEM((GROUPS * 16, 2 * ROWS), BF16),
            pltpu.VMEM((2 * ROWS, HD), F32),
            pltpu.VMEM((2 * ROWS, HD), F32),
            pltpu.VMEM((GROUPS, 16, 512), BF16),
            pltpu.VMEM((GROUPS, 16, H * HD // 2), BF16),
            pltpu.VMEM((GROUPS // 2, 2, 16, 512), BF16),
            pltpu.VMEM((GROUPS, 16, H * HD // 2), BF16),
            pltpu.VMEM((KVH, WIDE, HD), BF16),
            pltpu.VMEM((PIECES, KVH, 2, SLOTS, HD), BF16),
            pltpu.VMEM((2, SLOTS, WIDE), F32),
            pltpu.VMEM((SLOTS, HD), F32),
            pltpu.VMEM((KVH, 8, WIDE), F32),
            pltpu.VMEM((KVH, 8, WIDE), F32),
            pltpu.VMEM((KVH, HD, WIDE), F32),
            dma((2,)),
            dma((2,)),
            dma((2, 2)),
            dma((2,)),
            dma((2, 2, 3)),
            dma((2,)),
            dma((2, 2, 6)),
            dma((2, 2)),
            dma((2,)),
            dma((2,)),
            dma((2, HALF, KVH, 2)),
        ],
        compiler_params=pltpu.CompilerParams(
            collective_id=0, has_side_effects=True, vmem_limit_bytes=VMEM_BYTES
        ),
        name="attend",
    )(
        hidden.reshape(ROWS, -1),
        queries.reshape(ROWS, -1),
        key_weight,
        value_weight,
        lengths.reshape(1, -1),
        assign.reshape(1, -1),
        frequency,
    )
    return out.reshape(1, SLOTS, H * HD)


def solution(mesh):
    return jax.shard_map(
        per_device,
        mesh=mesh,
        in_specs=(
            P(None, "grp", "sp"),
            P(None, "grp", "sp"),
            P("sp", None),
            P("sp", None),
            P(),
            P(),
        ),
        out_specs=P("grp", None, "sp"),
        check_vma=False,
    )
```

```python
import jax
import jax.numpy as jnp
import numpy as np
from jax import lax
from jax.experimental import pallas as pl
from jax.experimental.pallas import tpu as pltpu
from jax.sharding import PartitionSpec as P

H = 16
KVH = 4
SHARE = H // KVH
HD = 128
GROUPS = 32
PIECES = 16
ROWS = 128
SLOTS = 192
HALF = PIECES // 2
WIDE = SHARE * SLOTS
FIRST = 2
ROPE_BASE = 500000.0
NEG_FILL = -1e30
LOG2E = 1.4426950408889634
MESH = pl.DeviceIdType.MESH
VMEM_BYTES = 56 * 1024 * 1024
F32 = jnp.float32
BF16 = jnp.bfloat16


def iota(shape, dim):
    return lax.broadcasted_iota(jnp.int32, shape, dim)


def kernel(
    hid_ref, q_ref, wk_ref, wv_ref, len_ref, asg_ref, freq_ref,
    o_ref,
    hid, qin, w, sel, cos, sin, kvp, qp, rkv, rq, qd, buf, bias, live, top, total, out_acc,
    in_sem, hid_sem, wz_sem, xa_send, xa_sem, xb_send, xb_sem,
    kv_sem, q_sem, ring_send, ring_recv,
):
    g = lax.axis_index("grp")
    z = lax.axis_index("sp")
    core = lax.rem(g, 2)
    chip = g // 2
    x = lax.rem(chip, 4)
    y = chip // 4
    zq = z // 4
    zm = lax.rem(z, 4)

    def loop(low, high, act):
        def body(k, carry):
            act(k)
            return carry

        lax.fori_loop(low, high, body, 0)

    barrier = pltpu.get_barrier_semaphore()

    def greet(device):
        pl.semaphore_signal(barrier, inc=1, device_id=device, device_id_type=MESH)

    loop(1, PIECES, lambda k: greet((g, lax.rem(z + k, PIECES))))
    loop(1, GROUPS, lambda k: greet((lax.rem(g + k, GROUPS), z)))

    hid_in = pltpu.make_async_copy(hid_ref, hid.at[core], in_sem.at[0])
    q_in = pltpu.make_async_copy(q_ref, qin, in_sem.at[1])
    hid_in.start()
    q_in.start()
    own_rows = pl.ds(pl.multiple_of(chip * 16, 16), 16)
    w[zq, zm, y, x] = jnp.where(core == 0, wk_ref[own_rows, :], wv_ref[own_rows, :])

    nseq = len_ref.shape[1]
    first = iota((nseq, nseq), 0)
    second = iota((nseq, nseq), 1)
    diagonal = first == second
    counts_r = (len_ref[...] // (GROUPS * PIECES)).astype(F32)
    asg_r = asg_ref[...].astype(F32)
    counts_c = jnp.sum(jnp.where(diagonal, counts_r, 0.0), axis=1, keepdims=True)
    asg_c = jnp.sum(jnp.where(diagonal, asg_r, 0.0), axis=1, keepdims=True)
    same_group = asg_c == asg_r
    up_c = jnp.where(first < second, counts_c, 0.0)
    up_r = jnp.where(second < first, counts_r, 0.0)
    starts_r = jnp.sum(up_c, axis=0, keepdims=True)
    starts_c = jnp.sum(up_r, axis=1, keepdims=True)
    offsets_r = jnp.sum(jnp.where(same_group, up_c, 0.0), axis=0, keepdims=True)
    offsets_c = jnp.sum(jnp.where(same_group, up_r, 0.0), axis=1, keepdims=True)

    pl.semaphore_wait(barrier, GROUPS - 1 + PIECES - 1)

    def heads_of(part):
        return (0, FIRST) if part == 0 else (FIRST, KVH)

    def cols(part):
        low, high = heads_of(part)
        return pl.ds(low * HD, (high - low) * HD)

    def rdma(src, dst, send, recv, device):
        return pltpu.make_async_remote_copy(
            src_ref=src, dst_ref=dst, send_sem=send, recv_sem=recv,
            device_id=device, device_id_type=MESH,
        )

    def wz(part, step):
        slab = w.at[zq, zm, y, x, :, cols(part)]
        return rdma(
            slab, slab, wz_sem.at[part, 0], wz_sem.at[part, 1],
            (g, lax.rem(z + step, PIECES)),
        )

    def take(ref, sem):
        pltpu.make_async_copy(ref, ref, sem).wait()

    def wz_take(part, way):
        take(kvp.at[0 : PIECES - 1, :, cols(part)], wz_sem.at[part, way])

    def x_peer(step):
        return (2 * (y * 4 + lax.rem(x + step, 4)) + core, z)

    def y_peer(step):
        return (2 * (lax.rem(y + step, 4) * 4 + x) + core, z)

    def xa(part, path, k):
        slab = w.at[2 * path : 2 * path + 2, :, y, x, :, cols(part)]
        return rdma(
            slab, slab, xa_send.at[part], xa_sem.at[part, path, k],
            (x_peer, y_peer)[path]((2, 1, 3)[k]),
        )

    def xb_view(part, path, shards, place):
        if path == 0:
            return w.at[shards, :, place, :, :, cols(part)]
        return w.at[shards, :, :, place, :, cols(part)]

    def xb(part, path, kind):
        place = (y, x)[path]
        peer = (y_peer, x_peer)[path]
        low = 2 * path
        one, two = slice(low, low + 1), slice(low + 1, low + 2)
        slab, device = (
            (xb_view(part, path, one, place), peer(1)),
            (xb_view(part, path, two, place), peer(3)),
            (xb_view(part, path, two, place), peer(1)),
            (xb_view(part, path, one, place), peer(3)),
            (xb_view(part, path, one, lax.rem(place + 3, 4)), peer(1)),
            (xb_view(part, path, two, lax.rem(place + 1, 4)), peer(3)),
        )[kind]
        return rdma(
            slab, slab, xb_send.at[part], xb_sem.at[part, path, kind], device
        )

    def xb_start(kinds, part):
        for path in range(2):
            for kind in kinds:
                xb(part, path, kind).start()

    def xb_wait(kinds, part):
        for path in range(2):
            for kind in kinds:
                xb(part, path, kind).wait_recv()

    def xb_relay(part):
        for path in range(2):
            xb(part, path, 0).wait_recv()
            xb(part, path, 4).start()
            xb(part, path, 1).wait_recv()
            xb(part, path, 5).start()

    def xa_start(part):
        for path in range(2):
            for k in range(3):
                xa(part, path, k).start()

    def xa_wait(part):
        for path in range(2):
            for k in range(3):
                xa(part, path, k).wait_recv()

    for part in range(2):
        for step in (8, 7, 9, 6, 10, 5, 11, 4, 12, 3, 13, 2, 14, 1, 15):
            wz(part, step).start()
    hid_in.wait()
    hid_copy = rdma(
        hid.at[core], hid.at[core], hid_sem.at[0], hid_sem.at[1], (g + 1 - 2 * core, z)
    )
    hid_copy.start()

    row_l = iota((nseq, ROWS), 1).astype(F32)
    here = (starts_c <= row_l) & (row_l < starts_c + counts_c)
    goal = jnp.sum(
        jnp.where(here, asg_c * 16.0 + offsets_c + row_l - starts_c, 0.0), axis=0, keepdims=True
    ).astype(jnp.int32)
    goal = jnp.concatenate([goal, goal + 8], axis=1)
    sel[...] = (iota((GROUPS * 16, 2 * ROWS), 0) == goal).astype(F32).astype(BF16)

    wz_take(0, 1)
    xa_start(0)
    row_s = iota((ROWS, nseq), 0).astype(F32)
    here = (starts_r <= row_s) & (row_s < starts_r + counts_r)
    base = jnp.sum(
        jnp.where(
            here,
            z.astype(F32) * counts_r * GROUPS + (row_s - starts_r) * GROUPS,
            0.0,
        ),
        axis=1, keepdims=True,
    )
    is_key = core == 0
    for lane in range(2):
        angles = (base + (2 * chip + lane).astype(F32)) * freq_ref[...]
        cosine = jnp.where(is_key, jnp.cos(angles), 1.0)
        sine = jnp.where(is_key, jnp.sin(angles), 0.0)
        at = pl.ds(lane * ROWS, ROWS)
        cos[at, :] = cosine
        sin[at, :] = jnp.where(iota((ROWS, HD), 1) < HD // 2, -sine, sine)
    wz_take(1, 1)
    xa_start(1)
    xa_wait(0)
    xb_start(range(4), 0)

    q_in.wait()
    q_cols = H * HD // 2
    qp[...] = (
        jnp.dot(sel[:, :ROWS], qin[:, :q_cols], preferred_element_type=F32)
        + jnp.dot(sel[:, ROWS:], qin[:, q_cols:], preferred_element_type=F32)
    ).astype(BF16).reshape(qp.shape)

    def project(part):
        low, high = heads_of(part)
        wide = (high - low) * HD
        sums = sum(
            jnp.dot(
                hid[:, :, s * 1024 : (s + 1) * 1024].reshape(2 * ROWS, 1024),
                w[s, :, :, :, :, cols(part)].reshape(1024, wide),
                preferred_element_type=F32,
            )
            for s in range(4)
        )
        for b in range(low, high):
            at = pl.ds(b * HD, HD)
            rows = sums[:, (b - low) * HD : (b - low + 1) * HD]
            turned = (rows * cos[...] + pltpu.roll(rows, HD // 2, 1) * sin[...]).astype(BF16)
            kvp[:, :, at] = (
                jnp.dot(sel[...], turned, preferred_element_type=F32)
                .astype(BF16)
                .reshape(GROUPS, 16, HD)
            )

    def kv_copy(part, k):
        peer = lax.rem(g + k, GROUPS)
        return rdma(
            kvp.at[peer, :, cols(part)], rkv.at[chip, core, :, cols(part)],
            kv_sem.at[part, 0], kv_sem.at[part, 1], (peer, z),
        )

    def kv_take(part, way):
        take(kvp.at[0 : GROUPS - 1, :, cols(part)], kv_sem.at[part, way])

    def q_copy(k):
        peer = lax.rem(g + k, GROUPS)
        return rdma(qp.at[peer], rq.at[g], q_sem.at[0], q_sem.at[1], (peer, z))

    def q_take(way):
        take(qp.at[0 : GROUPS - 1], q_sem.at[way])

    def kv_begin(part):
        loop(1, GROUPS, lambda k: kv_copy(part, k).start())
        rkv[chip, core, :, cols(part)] = kvp[g, :, cols(part)]

    def kv_end(part):
        low, high = heads_of(part)
        slot = iota((SLOTS, 256), 0)
        col = iota((SLOTS, 256), 1)
        unpack = (slot == (col & 7) * GROUPS + (col >> 3)).astype(F32).astype(BF16)
        kv_take(part, 1)
        for kind in range(2):
            dense = jnp.dot(
                unpack,
                rkv[:, kind, :, cols(part)].reshape(256, (high - low) * HD),
                preferred_element_type=F32,
            )
            for b in range(low, high):
                buf[z, b, kind] = dense[:, (b - low) * HD : (b - low + 1) * HD].astype(BF16)

    above = lax.rem(z + 1, PIECES)
    below = lax.rem(z + PIECES - 1, PIECES)

    def ring_copy(way, step, b, kind):
        if way == 0:
            piece, peer = lax.rem(z - step + PIECES, PIECES), above
        else:
            piece, peer = lax.rem(z + step, PIECES), below
        return rdma(
            buf.at[piece, b, kind], buf.at[piece, b, kind],
            ring_send.at[way], ring_recv.at[way, step, b, kind], (g, peer),
        )

    def arrival(way, step, b, kind):
        if way == 0:
            piece, peer = lax.rem(z - step - 1 + PIECES, PIECES), below
        else:
            piece, peer = lax.rem(z + step + 1, PIECES), above
        return rdma(
            buf.at[piece, b, kind], buf.at[piece, b, kind],
            ring_send.at[way], ring_recv.at[way, step, b, kind], (g, peer),
        )

    def ring_begin(part):
        for b in range(*heads_of(part)):
            for kind in range(2):
                ring_copy(0, 0, b, kind).start()
                ring_copy(1, 0, b, kind).start()

    def relay(step, b):
        on = step < HALF - 2
        for kind in range(2):
            for way in range(2):
                arrival(way, step, b, kind).wait_recv()
                if way == kind:
                    ring_copy(way, step + 1, b, kind).start()
                else:

                    @pl.when(on)
                    def _():
                        ring_copy(way, step + 1, b, kind).start()

    def last_wait(b):
        for kind in range(2):
            arrival(kind, HALF - 1, b, kind).wait_recv()

    scale = HD ** -0.5 * LOG2E

    def block(pieces, b, mask):
        queries = qd[b]
        scores = [
            lax.dot_general(
                buf[piece, b, 0], queries, (((1,), (1,)), ((), ())), preferred_element_type=F32
            )
            * scale
            + bias[mask]
            for piece in pieces
        ]
        high = jnp.max(scores[0], axis=0, keepdims=True)
        for each in scores[1:]:
            high = jnp.maximum(high, jnp.max(each, axis=0, keepdims=True))
        if mask == 0:
            old = top[b, 0:1]
            high = jnp.maximum(old, high)
            fade = jnp.exp2(old - high)
        weights = [jnp.exp2(each - high) for each in scores]
        added = sum(jnp.sum(each, axis=0, keepdims=True) for each in weights)
        part = sum(
            lax.dot_general(
                buf[piece, b, 1], each.astype(BF16), (((0,), (0,)), ((), ())),
                preferred_element_type=F32,
            )
            for piece, each in zip(pieces, weights)
        )
        top[b, 0:1] = high
        if mask == 0:
            total[b, 0:1] = total[b, 0:1] * fade + added
            out_acc[b] = out_acc[b] * fade + part
        else:
            total[b, 0:1] = added
            out_acc[b] = part

    def attend(step, b):
        lower = z - step - 1
        upper = z + step + 1 - PIECES

        @pl.when(upper >= 0)
        def _():
            block((lower, upper), b, 0)

        @pl.when((upper < 0) & (lower >= 0))
        def _():
            block((lower,), b, 0)

    def attend_last(b):
        @pl.when(z >= HALF)
        def _():
            block((z - HALF,), b, 0)

    def emit(b):
        rows = jnp.transpose(out_acc[b] * (1.0 / total[b, 0:1]))
        for h in range(SHARE):
            at = pl.ds(pl.multiple_of(b * (SHARE * HD), SHARE * HD) + h * HD, HD)
            o_ref[:, at] = jnp.where(
                live[...] > 0.5, rows[h * SLOTS : (h + 1) * SLOTS], 0.0
            ).astype(BF16)

    xb_relay(0)
    xa_wait(1)
    xb_start(range(4), 1)
    xb_wait(range(2, 6), 0)
    hid_copy.wait_recv()
    project(0)
    kv_begin(0)
    kv_end(0)
    ring_begin(0)
    xb_relay(1)
    loop(0, FIRST, lambda b: relay(0, b))

    unit_s = (iota((SLOTS, nseq), 0) >> 5).astype(F32)
    group = g.astype(F32)
    hit = (asg_r == group) & (offsets_r <= unit_s) & (unit_s < offsets_r + counts_r)
    seq_s = jnp.sum(
        jnp.where(hit, iota((SLOTS, nseq), 1) + 1, 0).astype(F32), axis=1, keepdims=True
    )

    def lane_slot(shape):
        lane = iota(shape, 1)
        for _ in range(SHARE - 1):
            lane = jnp.where(lane >= SLOTS, lane - SLOTS, lane)
        return lane

    unit_l = (lane_slot((nseq, WIDE)) >> 5).astype(F32)
    hit = (asg_c == group) & (offsets_c <= unit_l) & (unit_l < offsets_c + counts_c)
    seq_l = jnp.sum(
        jnp.where(hit, iota((nseq, WIDE), 0) + 1, 0).astype(F32), axis=0, keepdims=True
    )
    same = (seq_s == seq_l) & (seq_s > 0.5)
    bias[0] = jnp.where(same, 0.0, NEG_FILL)
    bias[1] = jnp.where(
        same & (iota((SLOTS, WIDE), 0) <= lane_slot((SLOTS, WIDE))), 0.0, NEG_FILL
    )
    live[...] = jnp.broadcast_to(seq_s, (SLOTS, HD))

    xb_wait(range(2, 6), 1)
    project(1)
    kv_begin(1)
    loop(0, FIRST, lambda b: relay(1, b))
    loop(0, FIRST, lambda b: relay(2, b))
    kv_end(1)
    ring_begin(1)
    loop(0, FIRST, lambda b: relay(3, b))
    loop(1, GROUPS, lambda k: q_copy(k).start())
    rq[g] = qp[g]
    loop(0, FIRST, lambda b: relay(4, b))
    loop(FIRST, KVH, lambda b: relay(0, b))
    loop(0, FIRST, lambda b: relay(5, b))
    loop(FIRST, KVH, lambda b: relay(1, b))
    loop(0, FIRST, lambda b: relay(6, b))
    q_take(1)
    arrived = rq[...].reshape(GROUPS * 16, q_cols)
    slot = iota((SLOTS, GROUPS * 16), 0)
    col = iota((SLOTS, GROUPS * 16), 1)
    for half in range(2):
        unpack = (slot == (col & 7) * GROUPS + (col >> 4)) & (((col >> 3) & 1) == half)
        dense = jnp.dot(unpack.astype(F32).astype(BF16), arrived, preferred_element_type=F32)
        for h in range(H // 2):
            head = half * (H // 2) + h
            qd[head // SHARE, pl.ds((head % SHARE) * SLOTS, SLOTS)] = dense[
                :, h * HD : (h + 1) * HD
            ].astype(BF16)

    loop(0, KVH, lambda b: block((z,), b, 1))

    rest = KVH - FIRST

    def steps(index):
        step = index // rest
        b = FIRST + lax.rem(index, rest)
        relay(step, b)
        attend(step - 2, b)

        @pl.when(b == FIRST)
        def _():
            loop(0, FIRST, lambda c: attend(step, c))

    loop(2 * rest, (HALF - 1) * rest, steps)
    loop(0, FIRST, lambda b: attend(0, b))
    loop(0, FIRST, lambda b: attend(1, b))
    for b in range(FIRST):
        last_wait(b)
        attend_last(b)
    loop(0, FIRST, emit)
    loop(FIRST, KVH, lambda b: attend(HALF - 3, b))
    loop(FIRST, KVH, lambda b: attend(HALF - 2, b))
    for b in range(FIRST, KVH):
        last_wait(b)
        attend_last(b)
    loop(FIRST, KVH, emit)

    hid_copy.wait_send()
    q_take(0)
    for part in range(2):
        wz_take(part, 0)
        kv_take(part, 0)
        take(w.at[0:3, :, :, 0, :, cols(part)], xa_send.at[part])
        take(w.at[0:3, :, :, :, :, cols(part)], xb_send.at[part])
    for way in range(2):
        take(buf.at[0 : HALF - 1], ring_send.at[way])
        take(buf.at[0, :, 0], ring_send.at[way])


def per_device(hidden, queries, key_weight, value_weight, lengths, assign):
    frequency = ROPE_BASE ** (-2.0 * np.arange(HD // 2) / HD)
    frequency = jnp.asarray(np.concatenate([frequency, frequency])[None], F32)
    vmem = pl.BlockSpec(memory_space=pltpu.VMEM)
    hbm = pl.BlockSpec(memory_space=pl.ANY)
    dma = pltpu.SemaphoreType.DMA
    out = pl.pallas_call(
        kernel,
        out_shape=jax.ShapeDtypeStruct((SLOTS, H * HD), BF16),
        in_specs=[hbm, hbm] + [vmem] * 5,
        out_specs=vmem,
        scratch_shapes=[
            pltpu.VMEM((2, ROWS, 4096), BF16),
            pltpu.VMEM((ROWS, H * HD), BF16),
            pltpu.VMEM((4, 4, 4, 4, 16, 512), BF16),
            pltpu.VMEM((GROUPS * 16, 2 * ROWS), BF16),
            pltpu.VMEM((2 * ROWS, HD), F32),
            pltpu.VMEM((2 * ROWS, HD), F32),
            pltpu.VMEM((GROUPS, 16, 512), BF16),
            pltpu.VMEM((GROUPS, 16, H * HD // 2), BF16),
            pltpu.VMEM((GROUPS // 2, 2, 16, 512), BF16),
            pltpu.VMEM((GROUPS, 16, H * HD // 2), BF16),
            pltpu.VMEM((KVH, WIDE, HD), BF16),
            pltpu.VMEM((PIECES, KVH, 2, SLOTS, HD), BF16),
            pltpu.VMEM((2, SLOTS, WIDE), F32),
            pltpu.VMEM((SLOTS, HD), F32),
            pltpu.VMEM((KVH, 8, WIDE), F32),
            pltpu.VMEM((KVH, 8, WIDE), F32),
            pltpu.VMEM((KVH, HD, WIDE), F32),
            dma((2,)),
            dma((2,)),
            dma((2, 2)),
            dma((2,)),
            dma((2, 2, 3)),
            dma((2,)),
            dma((2, 2, 6)),
            dma((2, 2)),
            dma((2,)),
            dma((2,)),
            dma((2, HALF, KVH, 2)),
        ],
        compiler_params=pltpu.CompilerParams(
            collective_id=0, has_side_effects=True, vmem_limit_bytes=VMEM_BYTES
        ),
        name="attend",
    )(
        hidden.reshape(ROWS, -1),
        queries.reshape(ROWS, -1),
        key_weight,
        value_weight,
        lengths.reshape(1, -1),
        assign.reshape(1, -1),
        frequency,
    )
    return out.reshape(1, SLOTS, H * HD)


def solution(mesh):
    return jax.shard_map(
        per_device,
        mesh=mesh,
        in_specs=(
            P(None, "grp", "sp"),
            P(None, "grp", "sp"),
            P("sp", None),
            P("sp", None),
            P(),
            P(),
        ),
        out_specs=P("grp", None, "sp"),
        check_vma=False,
    )
```
